32 devices in a mesh: member: 2 (over x), dom: 16 (over z, y, core).
Axes of the slice: x: 2, y: 2, z: 4, core: 2. Of those that a mesh axis runs over, the one named last changes fastest.
Arguments:
- node_latent: bfloat16 [16384, 512], P(('member', 'dom')), parts along dimension 0, may hold values from -6 to 6
- edge_latent: bfloat16 [81920, 512], P(('member', 'dom')), parts along dimension 0, may hold values from -6 to 6
- node_cotan: bfloat16 [16384, 512], P(('member', 'dom')), parts along dimension 0, may hold values from -6 to 6
- edge_cotan: bfloat16 [81920, 512], P(('member', 'dom')), parts along dimension 0, may hold values from -6 to 6
- edge_w1: bfloat16 [1536, 512], replicated, may hold values from -0.15625 to 0.15625
- edge_w2: bfloat16 [512, 512], replicated, may hold values from -0.25 to 0.25
- node_w1: bfloat16 [1024, 512], replicated, may hold values from -0.1875 to 0.1875
- node_w2: bfloat16 [512, 512], replicated, may hold values from -0.25 to 0.25
- send_rows: int32 [16, 16, 16], P('dom'), may hold values from 0 to 511, as said below
- senders: int32 [40960], P('dom'), may hold values from 0 to 767, as said below
- receivers: int32 [40960], P('dom'), may hold values from 0 to 511, as said below
- edge_count: int32 [16], P('dom'), may hold values from 640 to 2560, as said below
Outputs:
- grad_node: float32 [16384, 512], P(('member', 'dom')), parts along dimension 0
- grad_edge: bfloat16 [81920, 512], P(('member', 'dom')), parts along dimension 0
- edge_weight_grads: float32 [4096, 512], P(('member', 'dom')), parts along dimension 0
- node_weight_grads: float32 [3072, 512], P(('member', 'dom')), parts along dimension 0
The draws below stay inside these ranges and needn't reach their ends.
There are 2 independent parts, one for each index of `member`. The reference program is written for one: setup_inputs(seed, part) draws one part's arguments, and reference() takes and returns one part's arrays. A program takes and returns all parts, laid end to end along the dimension named above; an argument that names none is the same for every part. Nothing has to cross between parts.
Inputs may be any that keep to these rules, and one draw needn't show every extreme that they name: `send_rows`: row of the sending partition's 512 nodes. `senders`: below 512: a node of the edge's own partition; else k - 512 names slot (k - 512) % 16 received from partition (k - 512) // 16. `receivers`: a node of the edge's own partition; non-decreasing within the rows of one partition. A partition's live edges are its first edge_count slots; some partition has all 2560 live.
All inputs are finite; a program needn't handle non-finite values.
Results may differ from the reference program's by a relative error of at most 0.0075.
Values may be sent and summed in bfloat16 or wider, within the bound.
No kernel may reach another device: no remote copies, remote signals or barrier semaphores. Data moves between devices by JAX's collectives and lax.ppermute only.
A program may use at most 128 MiB of HBM per device.

```python
import jax
import jax.numpy as jnp
from jax import lax

D = 512
NODE_DEV = 512
EDGE_DEV = 2560
SLOT = 16
NODES = 8192
EDGES = 40960
N_DOM = 16


def draw_send_rows(key, part):
    key = jax.random.fold_in(key, 11)
    rows_drawn = jax.random.randint(key, (N_DOM, N_DOM, SLOT), 0, NODE_DEV, dtype=jnp.int32)
    rows_drawn = rows_drawn.at[0, 0, 0].set(NODE_DEV - 1)
    rows_drawn = rows_drawn.at[N_DOM - 1, 0, SLOT - 1].set(0)
    return rows_drawn


def draw_senders(key, part):
    key = jax.random.fold_in(key, 12)
    first, second, third = jax.random.split(key, 3)
    local_rows = jax.random.randint(first, (EDGES,), 0, NODE_DEV, dtype=jnp.int32)
    remote_rows = NODE_DEV + jax.random.randint(second, (EDGES,), 0, N_DOM * SLOT, dtype=jnp.int32)
    choose = jax.random.randint(third, (EDGES,), 0, 2, dtype=jnp.int32)
    drawn = jnp.where(choose == 1, remote_rows, local_rows)
    place = jnp.arange(EDGES, dtype=jnp.int32) % EDGE_DEV
    drawn = jnp.where(place == 1, NODE_DEV + N_DOM * SLOT - 1, drawn)
    drawn = jnp.where(place == 0, 0, drawn)
    return drawn.astype(jnp.int32)


def draw_receivers(key, part):
    key = jax.random.fold_in(key, 13)
    drawn = jax.random.randint(key, (N_DOM, EDGE_DEV), 0, NODE_DEV, dtype=jnp.int32)
    drawn = jnp.sort(drawn, axis=1)
    drawn = drawn.at[:, 0].set(0)
    drawn = drawn.at[:, EDGE_DEV - 1].set(NODE_DEV - 1)
    return drawn.reshape(EDGES).astype(jnp.int32)


def draw_edge_count(key, part):
    key = jax.random.fold_in(key, 14)
    first, second = jax.random.split(key)
    counts = jax.random.randint(first, (N_DOM,), EDGE_DEV // 4, EDGE_DEV + 1, dtype=jnp.int32)
    fullest = jax.random.randint(second, (), 0, N_DOM, dtype=jnp.int32)
    counts = jnp.where(jnp.arange(N_DOM, dtype=jnp.int32) == fullest, EDGE_DEV, counts)
    counts = counts.at[(fullest + 1) % N_DOM].set(EDGE_DEV // 4)
    return counts.astype(jnp.int32)


def block_levels(stream_key, dims, shards, low, largest):
    loudness = 1.0
    for position, parts in shards:
        heights = jax.random.uniform(jax.random.fold_in(jax.random.fold_in(stream_key, 6), position), (parts,), jnp.float32, low / len(shards), largest / len(shards))
        loudness = loudness * jnp.repeat(jnp.exp(heights), dims[position] // parts).reshape((-1,) + (1,) * (len(dims) - 1 - position))
    return loudness


def noise(rng, dims, spread, most, pieces=(), kind=jnp.bfloat16):
    loudness = block_levels(rng, dims, pieces, -0.22, 0.18) if pieces else 1.0
    entries = jax.random.normal(rng, dims, jnp.float32) * spread * loudness
    return jnp.minimum(jnp.maximum(entries, -most), most).astype(kind)


def setup_inputs(seed: int = 0, part: int = 0) -> dict:
    key_of = jax.random.split(jax.random.key(seed), 13)
    own_keys = jax.random.split(jax.random.fold_in(key_of[12], part), 13)
    node_latent = noise(own_keys[0], (NODES, D), 1.0, 6.0, ((0, 16),))
    edge_latent = noise(own_keys[1], (EDGES, D), 1.0, 6.0, ((0, 16),))
    node_cotan = noise(own_keys[2], (NODES, D), 1.0, 6.0, ((0, 16),))
    edge_cotan = noise(own_keys[3], (EDGES, D), 1.0, 6.0, ((0, 16),))
    edge_w1 = noise(key_of[4], (3 * D, D), (3 * D) ** -0.5, 0.15625)
    edge_w2 = noise(key_of[5], (D, D), D ** -0.5, 0.25)
    node_w1 = noise(key_of[6], (2 * D, D), (2 * D) ** -0.5, 0.1875)
    node_w2 = noise(key_of[7], (D, D), D ** -0.5, 0.25)
    send_rows = draw_send_rows(jax.random.fold_in(key_of[12], 71), part)
    senders = draw_senders(jax.random.fold_in(key_of[12], 71), part)
    receivers = draw_receivers(jax.random.fold_in(key_of[12], 71), part)
    edge_count = draw_edge_count(jax.random.fold_in(key_of[12], 71), part)
    return dict(node_latent=node_latent, edge_latent=edge_latent, node_cotan=node_cotan, edge_cotan=edge_cotan, edge_w1=edge_w1, edge_w2=edge_w2, node_w1=node_w1, node_w2=node_w2, send_rows=send_rows, senders=senders, receivers=receivers, edge_count=edge_count)


def swish_value(value):
    return value * jax.nn.sigmoid(value)

def swish_slope(value):
    sig = jax.nn.sigmoid(value)
    return sig * (1.0 + value * (1.0 - sig))

def normalize(mixed):
    centre = mixed - lax.optimization_barrier(jnp.mean(mixed, -1, keepdims=True))
    inverse = lax.rsqrt(lax.optimization_barrier(jnp.mean(centre * centre, -1, keepdims=True)) + 1e-05)
    return (centre * inverse, inverse)

def norm_back(grad, normed, inverse):
    return inverse * (grad - lax.optimization_barrier(jnp.mean(grad, -1, keepdims=True)) - normed * lax.optimization_barrier(jnp.mean(grad * normed, -1, keepdims=True)))

def product(left, right):
    return jnp.dot(left, right, preferred_element_type=jnp.float32)

def contract_rows(left, right):
    return lax.dot_general(left, right, (((0,), (0,)), ((), ())), preferred_element_type=jnp.float32)

def times_transpose(left, weight):
    return lax.dot_general(left, weight, (((1,), (1,)), ((), ())), preferred_element_type=jnp.float32)

def reference(node_latent, edge_latent, node_cotan, edge_cotan, edge_w1, edge_w2, node_w1, node_w2, send_rows, senders, receivers, edge_count):
    place = jnp.arange(EDGES, dtype=jnp.int32)
    owner = place // EDGE_DEV
    live_mask = (place % EDGE_DEV < edge_count[owner]).astype(jnp.float32)[:, None]
    slot_index = jnp.maximum(senders - NODE_DEV, 0)
    peer_index = slot_index // SLOT
    within = slot_index % SLOT
    far_row = send_rows[peer_index, owner, within]
    sender_id = jnp.where(senders < NODE_DEV, owner * NODE_DEV + senders, peer_index * NODE_DEV + far_row).astype(jnp.int32)
    recv_id = (owner * NODE_DEV + receivers).astype(jnp.int32)
    w_send = edge_w1[:D]
    w_recv = edge_w1[D:2 * D]
    w_edge = edge_w1[2 * D:]
    w_node = node_w1[:D]
    w_agg = node_w1[D:]
    send_x = node_latent[sender_id]
    recv_x = node_latent[recv_id]
    edge_pre = product(send_x, w_send) + product(recv_x, w_recv) + product(edge_latent, w_edge)
    edge_hidden = swish_value(edge_pre).astype(jnp.bfloat16)
    edge_normed, edge_inv = normalize(product(edge_hidden, edge_w2))
    message = (live_mask * edge_normed).astype(jnp.bfloat16)
    gathered = jax.ops.segment_sum(message.astype(jnp.float32), recv_id, num_segments=NODES).astype(jnp.bfloat16)
    node_pre = product(node_latent, w_node) + product(gathered, w_agg)
    node_hidden = swish_value(node_pre).astype(jnp.bfloat16)
    node_normed, node_inv = normalize(product(node_hidden, node_w2))
    node_grad_out = norm_back(node_cotan.astype(jnp.float32), node_normed, node_inv).astype(jnp.bfloat16)
    node_grad_pre = (times_transpose(node_grad_out, node_w2) * swish_slope(node_pre)).astype(jnp.bfloat16)
    node_weight_grads = jnp.concatenate([contract_rows(node_latent, node_grad_pre), contract_rows(gathered, node_grad_pre), contract_rows(node_hidden, node_grad_out)], 0)
    agg_grad = times_transpose(node_grad_pre, w_agg).astype(jnp.bfloat16)
    grad_msg = live_mask * (edge_cotan.astype(jnp.float32) + agg_grad[recv_id].astype(jnp.float32))
    edge_grad_mixed = norm_back(grad_msg, edge_normed, edge_inv).astype(jnp.bfloat16)
    edge_grad_pre = (times_transpose(edge_grad_mixed, edge_w2) * swish_slope(edge_pre)).astype(jnp.bfloat16)
    edge_weight_grads = jnp.concatenate([contract_rows(send_x, edge_grad_pre), contract_rows(recv_x, edge_grad_pre), contract_rows(edge_latent, edge_grad_pre), contract_rows(edge_hidden, edge_grad_mixed)], 0)
    grad_edge = (edge_cotan.astype(jnp.float32) + times_transpose(edge_grad_pre, w_edge)).astype(jnp.bfloat16)
    grad_send = times_transpose(edge_grad_pre, w_send).astype(jnp.bfloat16)
    grad_recv = times_transpose(edge_grad_pre, w_recv).astype(jnp.bfloat16)
    grad_node = node_cotan.astype(jnp.float32) + times_transpose(node_grad_pre, w_node)
    grad_node = grad_node + jax.ops.segment_sum(grad_send.astype(jnp.float32), sender_id, num_segments=NODES)
    grad_node = grad_node + jax.ops.segment_sum(grad_recv.astype(jnp.float32), recv_id, num_segments=NODES)
    return (grad_node, grad_edge, edge_weight_grads, node_weight_grads)
```

```python
import functools

import jax
import jax.numpy as jnp
from jax import lax
from jax.experimental import pallas as pl
from jax.experimental.pallas import tpu as pltpu
from jax.sharding import PartitionSpec as P

BF = jnp.bfloat16
F32 = jnp.float32
VMEM_BYTES = 56 * 1024 * 1024


def dot(left, right):
    return jnp.dot(left, right, preferred_element_type=F32)


def dot_rows(left, right):
    return lax.dot_general(left, right, (((0,), (0,)), ((), ())), preferred_element_type=F32)


def dot_last(left, right):
    return lax.dot_general(left, right, (((1,), (1,)), ((), ())), preferred_element_type=F32)


def split(value):
    high = value.astype(BF)
    return high, (value - high.astype(F32)).astype(BF)


def pick(row, base, count):
    size = row.shape[1]
    column = jnp.broadcast_to(row, (128, size)).T
    wide = jnp.concatenate([column] * (count // 128), 1)
    place = lax.broadcasted_iota(jnp.int32, (size, count), 1) + base
    return jnp.where(wide == place, 1.0, 0.0).astype(BF)


def pick_t(row, base, count):
    size = row.shape[1]
    place = lax.broadcasted_iota(jnp.int32, (count, size), 0) + base
    return jnp.where(jnp.broadcast_to(row, (count, size)) == place, 1.0, 0.0).astype(BF)


def normalize(mixed):
    centre = mixed - jnp.mean(mixed, -1, keepdims=True)
    inverse = lax.rsqrt(jnp.mean(centre * centre, -1, keepdims=True) + 1e-05)
    return centre * inverse, inverse


def norm_back(grad, normed, inverse):
    return inverse * (
        grad
        - jnp.mean(grad, -1, keepdims=True)
        - normed * jnp.mean(grad * normed, -1, keepdims=True)
    )


def swish_both(value):
    sig = jax.nn.sigmoid(value)
    hidden = value * sig
    return hidden.astype(BF), sig * (1.0 + value * (1.0 - sig))


def rows_kernel(rows_ref, latent_ref, out_ref):
    out_ref[...] = dot(pick(rows_ref[...], 0, latent_ref.shape[0]), latent_ref[...]).astype(BF)


def early_kernel(send_ref, recv_ref, edge_ref, latent_ref, w1_ref, pre_ref, high, low):
    nodes, width = latent_ref.shape

    @pl.when(pl.program_id(0) == 0)
    def _():
        latent = latent_ref[...]
        for part in range(2):
            table_high, table_low = split(dot(latent, w1_ref[pl.ds(part * width, width), :]))
            high[pl.ds(part * nodes, nodes), :] = table_high
            low[pl.ds(part * nodes, nodes), :] = table_low

    both = jnp.concatenate([pick(send_ref[0], 0, nodes), pick(recv_ref[0], 0, nodes)], 1)
    pre_ref[...] = (
        dot(edge_ref[...], w1_ref[pl.ds(2 * width, width), :])
        + dot(both, high[...])
        + dot(both, low[...])
    )


def stash(acc, row0, keep_ref, send_ref, core):
    groups, rows, _ = keep_ref.shape
    for group in range(groups):
        mine = pl.multiple_of(row0 + (2 * group + core) * rows, 16)
        other = pl.multiple_of(row0 + (2 * group + 1 - core) * rows, 16)
        keep_ref[group] = acc[pl.ds(mine, rows), :]
        send_ref[group] = acc[pl.ds(other, rows), :].astype(BF)


def forward_kernel(
    scalar_ref, send_ref, recv_ref, pre_ref, halo_ref, wsend_ref, w2_ref,
    latent_ref, cotan_ref, nw1_ref, nw2_ref,
    hidden_ref, slope_ref, normed_ref, inverse_ref, agg_ref, grad_ref, keep_ref, away_ref,
    table, gathered, acc,
):
    turn = pl.program_id(0)
    nodes, width = latent_ref.shape
    halo = halo_ref.shape[0]
    size = pre_ref.shape[0]

    @pl.when(turn == 0)
    def _():
        high, low = split(dot(halo_ref[...], wsend_ref[...]))
        table[pl.ds(0, halo), :] = high
        table[pl.ds(halo, halo), :] = low
        gathered[...] = jnp.zeros_like(gathered)

    far = pick(send_ref[0], nodes, halo)
    pre = pre_ref[...] + dot(far, table[pl.ds(0, halo), :]) + dot(far, table[pl.ds(halo, halo), :])
    hidden, slope = swish_both(pre)
    hidden_ref[...] = hidden
    slope_ref[...] = slope
    normed, inverse = normalize(dot(hidden, w2_ref[...]))
    normed_ref[...] = normed
    inverse_ref[...] = inverse
    place = turn * size + lax.broadcasted_iota(jnp.int32, (size, 1), 0)
    message = jnp.where(place < scalar_ref[0], normed, 0.0).astype(BF)
    gathered[...] += dot(pick_t(recv_ref[0], 0, nodes), message)

    @pl.when(turn == pl.num_programs(0) - 1)
    def _():
        latent = latent_ref[...]
        sums = gathered[...].astype(BF)
        w_node = nw1_ref[pl.ds(0, width), :]
        w_agg = nw1_ref[pl.ds(width, width), :]
        node_hidden, node_slope = swish_both(dot(latent, w_node) + dot(sums, w_agg))
        node_normed, node_inverse = normalize(dot(node_hidden, nw2_ref[...]))
        cotan = cotan_ref[...].astype(F32)
        grad_out = norm_back(cotan, node_normed, node_inverse).astype(BF)
        grad_pre = (dot_last(grad_out, nw2_ref[...]) * node_slope).astype(BF)
        agg_ref[...] = dot_last(grad_pre, w_agg).astype(BF)
        grad_ref[...] = cotan + dot_last(grad_pre, w_node)
        acc[pl.ds(0, width), :] = dot_rows(latent, grad_pre)
        acc[pl.ds(width, width), :] = dot_rows(sums, grad_pre)
        acc[pl.ds(2 * width, width), :] = dot_rows(node_hidden, grad_out)
        stash(acc, 0, keep_ref, away_ref, scalar_ref[1])


def backward_kernel(
    scalar_ref, send_ref, recv_ref, edge_ref, cotan_ref, hidden_ref, slope_ref, normed_ref, inverse_ref,
    agg_ref, grad_ref, latent_ref, halo_ref, w1_ref, w2_ref,
    edge_out, node_out, far_out, keep_ref, away_ref,
    sent, received, acc,
):
    turn = pl.program_id(0)
    nodes, width = latent_ref.shape
    halo = halo_ref.shape[0]
    size = edge_ref.shape[0]

    @pl.when(turn == 0)
    def _():
        sent[...] = jnp.zeros_like(sent)
        received[...] = jnp.zeros_like(received)
        acc[...] = jnp.zeros_like(acc)

    recv_row = recv_ref[0]
    cotan = cotan_ref[...].astype(F32)
    place = turn * size + lax.broadcasted_iota(jnp.int32, (size, 1), 0)
    grad_msg = jnp.where(
        place < scalar_ref[0], cotan + dot(pick(recv_row, 0, nodes), agg_ref[...]), 0.0
    )
    grad_mixed = norm_back(grad_msg, normed_ref[...], inverse_ref[...]).astype(BF)
    grad_pre = (dot_last(grad_mixed, w2_ref[...]) * slope_ref[...]).astype(BF)
    acc[pl.ds(3 * width, width), :] += dot_rows(hidden_ref[...], grad_mixed)
    acc[pl.ds(2 * width, width), :] += dot_rows(edge_ref[...], grad_pre)
    sent[...] += dot(pick_t(send_ref[0], 0, nodes + halo), grad_pre)
    received[...] += dot(pick_t(recv_row, 0, nodes), grad_pre)
    edge_out[...] = (cotan + dot_last(grad_pre, w1_ref[pl.ds(2 * width, width), :])).astype(BF)

    @pl.when(turn == pl.num_programs(0) - 1)
    def _():
        w_send = w1_ref[pl.ds(0, width), :]
        latent = latent_ref[...]
        near = sent[pl.ds(0, nodes), :].astype(BF)
        far = sent[pl.ds(nodes, halo), :].astype(BF)
        into = received[...].astype(BF)
        far_out[...] = dot_last(far, w_send).astype(BF)
        node_out[...] = (
            grad_ref[...] + dot_last(near, w_send) + dot_last(into, w1_ref[pl.ds(width, width), :])
        )
        acc[pl.ds(0, width), :] = dot_rows(latent, near) + dot_rows(halo_ref[...], far)
        acc[pl.ds(width, width), :] = dot_rows(latent, into)
        stash(acc, 0, keep_ref, away_ref, scalar_ref[1])


def return_kernel(rows_ref, back_ref, part_ref, out_ref):
    out_ref[...] = part_ref[...] + dot(pick_t(rows_ref[...], 0, out_ref.shape[0]), back_ref[...])


def whole(shape):
    return pl.BlockSpec(shape, lambda i: (0,) * len(shape))


def by_rows(size, width):
    return pl.BlockSpec((size, width), lambda i: (i, 0))


def reduce_scatter(keep, away, count):
    place = lax.axis_index("dom")
    _, rows, width = keep.shape
    total = keep + lax.ppermute(away, "dom", [(i, i ^ 1) for i in range(count)]).astype(F32)
    groups = count // 4
    total = total.reshape(groups, 2, rows, width)
    side = (place // 2) % 2
    mine = lax.dynamic_index_in_dim(total, side, 1, keepdims=False)
    other = lax.dynamic_index_in_dim(total, 1 - side, 1, keepdims=False).astype(BF)
    total = mine + lax.ppermute(other, "dom", [(i, i ^ 2) for i in range(count)]).astype(F32)
    group = place // 4
    result = lax.dynamic_index_in_dim(total, group, 0, keepdims=False)
    for step in range(1, groups):
        piece = lax.dynamic_index_in_dim(total, (group + step) % groups, 0, keepdims=False).astype(BF)
        result = result + lax.ppermute(
            piece, "dom", [(i, (i + 4 * step) % count) for i in range(count)]
        ).astype(F32)
    return result


def local(
    count,
    node_latent,
    edge_latent,
    node_cotan,
    edge_cotan,
    edge_w1,
    edge_w2,
    node_w1,
    node_w2,
    send_rows,
    senders,
    receivers,
    edge_count,
):
    nodes, width = node_latent.shape
    edges = edge_latent.shape[0]
    peers, slots = send_rows.shape[1:]
    halo = peers * slots
    size = 512
    turns = edges // size
    place = lax.axis_index("dom")
    scalars = jnp.stack([edge_count[0], (place % 2).astype(jnp.int32)])
    flat_rows = send_rows.reshape(1, halo)
    send_row = senders.reshape(turns, 1, size)
    recv_row = receivers.reshape(turns, 1, size)
    row_spec = pl.BlockSpec((1, 1, size), lambda i: (i, 0, 0))
    smem = pl.BlockSpec(memory_space=pltpu.SMEM)
    params = pltpu.CompilerParams(vmem_limit_bytes=VMEM_BYTES)
    unit = 2 * edges * width * width

    def cost(units, bytes_accessed):
        return pl.CostEstimate(flops=int(units * unit), bytes_accessed=bytes_accessed, transcendentals=0)

    outgoing = pl.pallas_call(
        rows_kernel,
        out_shape=jax.ShapeDtypeStruct((halo, width), BF),
        compiler_params=params,
        cost_estimate=cost(0.1, 3 * halo * width * 2),
        name="halo_rows",
    )(flat_rows, node_latent)
    incoming = lax.all_to_all(
        outgoing.reshape(peers, slots, width), "dom", split_axis=0, concat_axis=0, tiled=True
    ).reshape(halo, width)

    pre = pl.pallas_call(
        early_kernel,
        grid=(turns,),
        in_specs=[row_spec, row_spec, by_rows(size, width), whole((nodes, width)), whole(edge_w1.shape)],
        out_specs=by_rows(size, width),
        out_shape=jax.ShapeDtypeStruct((edges, width), F32),
        scratch_shapes=[pltpu.VMEM((2 * nodes, width), BF)] * 2,
        compiler_params=params,
        cost_estimate=cost(5.5, edges * width * 6),
        name="edge_early",
    )(send_row, recv_row, edge_latent, node_latent, edge_w1)

    node_rows = 3 * width // count
    edge_rows = 4 * width // count
    hidden, slope, normed, inverse, agg_grad, grad_part, node_keep, node_away = pl.pallas_call(
        forward_kernel,
        grid=(turns,),
        in_specs=[
            smem, row_spec, row_spec, by_rows(size, width), whole((halo, width)), whole((width, width)),
            whole((width, width)), whole((nodes, width)), whole((nodes, width)),
            whole(node_w1.shape), whole(node_w2.shape),
        ],
        out_specs=[
            by_rows(size, width), by_rows(size, width), by_rows(size, width), by_rows(size, 1),
            whole((nodes, width)), whole((nodes, width)),
            whole((count // 2, node_rows, width)), whole((count // 2, node_rows, width)),
        ],
        out_shape=[
            jax.ShapeDtypeStruct((edges, width), BF),
            jax.ShapeDtypeStruct((edges, width), F32),
            jax.ShapeDtypeStruct((edges, width), F32),
            jax.ShapeDtypeStruct((edges, 1), F32),
            jax.ShapeDtypeStruct((nodes, width), BF),
            jax.ShapeDtypeStruct((nodes, width), F32),
            jax.ShapeDtypeStruct((count // 2, node_rows, width), F32),
            jax.ShapeDtypeStruct((count // 2, node_rows, width), BF),
        ],
        scratch_shapes=[
            pltpu.VMEM((2 * halo, width), BF),
            pltpu.VMEM((nodes, width), F32),
            pltpu.VMEM((3 * width, width), F32),
        ],
        compiler_params=params,
        cost_estimate=cost(6, edges * width * 20),
        name="edge_forward",
    )(
        scalars, send_row, recv_row, pre, incoming, edge_w1, edge_w2,
        node_latent, node_cotan, node_w1, node_w2,
    )

    node_share = reduce_scatter(node_keep, node_away, count)

    grad_edge, node_part, far_grad, edge_keep, edge_away = pl.pallas_call(
        backward_kernel,
        grid=(turns,),
        in_specs=[
            smem, row_spec, row_spec, by_rows(size, width), by_rows(size, width), by_rows(size, width),
            by_rows(size, width), by_rows(size, width), by_rows(size, 1),
            whole((nodes, width)), whole((nodes, width)), whole((nodes, width)), whole((halo, width)),
            whole(edge_w1.shape), whole(edge_w2.shape),
        ],
        out_specs=[
            by_rows(size, width), whole((nodes, width)), whole((halo, width)),
            whole((count // 2, edge_rows, width)), whole((count // 2, edge_rows, width)),
        ],
        out_shape=[
            jax.ShapeDtypeStruct((edges, width), BF),
            jax.ShapeDtypeStruct((nodes, width), F32),
            jax.ShapeDtypeStruct((halo, width), BF),
            jax.ShapeDtypeStruct((count // 2, edge_rows, width), F32),
            jax.ShapeDtypeStruct((count // 2, edge_rows, width), BF),
        ],
        scratch_shapes=[
            pltpu.VMEM((nodes + halo, width), F32),
            pltpu.VMEM((nodes, width), F32),
            pltpu.VMEM((4 * width, width), F32),
        ],
        compiler_params=params,
        cost_estimate=cost(10, edges * width * 20),
        name="edge_backward",
    )(
        scalars, send_row, recv_row, edge_latent, edge_cotan, hidden, slope, normed, inverse,
        agg_grad, grad_part, node_latent, incoming, edge_w1, edge_w2,
    )

    returned = lax.all_to_all(
        far_grad.reshape(peers, slots, width), "dom", split_axis=0, concat_axis=0, tiled=True
    ).reshape(halo, width)
    edge_share = reduce_scatter(edge_keep, edge_away, count)
    grad_node = pl.pallas_call(
        return_kernel,
        out_shape=jax.ShapeDtypeStruct((nodes, width), F32),
        compiler_params=params,
        cost_estimate=cost(0.1, nodes * width * 8),
        name="halo_return",
    )(flat_rows, returned, node_part)
    return (grad_node, grad_edge, edge_share, node_share)


def solution(mesh):
    rows = P(("member", "dom"), None)
    placed = (
        rows, rows, rows, rows, P(), P(), P(), P(), P("dom", None, None), P("dom"), P("dom"), P("dom"),
    )
    return jax.shard_map(
        functools.partial(local, mesh.shape["dom"]),
        mesh=mesh,
        in_specs=placed,
        out_specs=(rows, rows, rows, rows),
        check_vma=False,
    )
```

```python
import functools

import jax
import jax.numpy as jnp
from jax import lax
from jax.experimental import pallas as pl
from jax.experimental.pallas import tpu as pltpu
from jax.sharding import PartitionSpec as P

BF = jnp.bfloat16
F32 = jnp.float32
VMEM_BYTES = 56 * 1024 * 1024


def dot(left, right):
    return jnp.dot(left, right, preferred_element_type=F32)


def dot_rows(left, right):
    return lax.dot_general(left, right, (((0,), (0,)), ((), ())), preferred_element_type=F32)


def dot_last(left, right):
    return lax.dot_general(left, right, (((1,), (1,)), ((), ())), preferred_element_type=F32)


def split(value):
    high = value.astype(BF)
    return high, (value - high.astype(F32)).astype(BF)


def pick(row, base, count):
    size = row.shape[1]
    column = jnp.broadcast_to(row, (128, size)).T
    wide = jnp.concatenate([column] * (count // 128), 1)
    place = lax.broadcasted_iota(jnp.int32, (size, count), 1) + base
    return jnp.where(wide == place, 1.0, 0.0).astype(BF)


def pick_t(row, base, count):
    size = row.shape[1]
    place = lax.broadcasted_iota(jnp.int32, (count, size), 0) + base
    return jnp.where(jnp.broadcast_to(row, (count, size)) == place, 1.0, 0.0).astype(BF)


def normalize(mixed):
    centre = mixed - jnp.mean(mixed, -1, keepdims=True)
    inverse = lax.rsqrt(jnp.mean(centre * centre, -1, keepdims=True) + 1e-05)
    return centre * inverse, inverse


def norm_back(grad, normed, inverse):
    return inverse * (
        grad
        - jnp.mean(grad, -1, keepdims=True)
        - normed * jnp.mean(grad * normed, -1, keepdims=True)
    )


def swish_both(value):
    sig = jax.nn.sigmoid(value)
    hidden = value * sig
    return hidden.astype(BF), sig * (1.0 + value * (1.0 - sig))


def rows_kernel(rows_ref, latent_ref, out_ref):
    out_ref[...] = dot(pick(rows_ref[...], 0, latent_ref.shape[0]), latent_ref[...]).astype(BF)


def early_kernel(send_ref, recv_ref, edge_ref, latent_ref, w1_ref, pre_ref, high, low):
    nodes, width = latent_ref.shape

    @pl.when(pl.program_id(0) == 0)
    def _():
        latent = latent_ref[...]
        for part in range(2):
            table_high, table_low = split(dot(latent, w1_ref[pl.ds(part * width, width), :]))
            high[pl.ds(part * nodes, nodes), :] = table_high
            low[pl.ds(part * nodes, nodes), :] = table_low

    size = edge_ref.shape[0]
    both = jnp.concatenate(
        [pick(block_row(send_ref, size), 0, nodes), pick(block_row(recv_ref, size), 0, nodes)], 1
    )
    pre_ref[...] = (
        dot(edge_ref[...], w1_ref[pl.ds(2 * width, width), :])
        + dot(both, high[...])
        + dot(both, low[...])
    )


def block_row(ref, size):
    return ref[pl.ds(pl.multiple_of(pl.program_id(0) * size, size), size)].reshape(1, size)


def accumulate(acc, value):
    @pl.when(pl.program_id(0) == 0)
    def _():
        acc[...] = value

    @pl.when(pl.program_id(0) > 0)
    def _():
        acc[...] += value


def stash(acc, row0, keep_ref, send_ref, core):
    groups, rows, _ = keep_ref.shape
    for group in range(groups):
        mine = pl.multiple_of(row0 + (2 * group + core) * rows, 16)
        other = pl.multiple_of(row0 + (2 * group + 1 - core) * rows, 16)
        keep_ref[group] = acc[pl.ds(mine, rows), :]
        send_ref[group] = acc[pl.ds(other, rows), :].astype(BF)


def forward_kernel(
    scalar_ref, send_ref, recv_ref, pre_ref, halo_ref, wsend_ref, w2_ref,
    latent_ref, cotan_ref, nw1_ref, nw2_ref,
    hidden_ref, slope_ref, normed_ref, inverse_ref, agg_ref, grad_ref, keep_ref, away_ref,
    table, gathered, acc,
):
    turn = pl.program_id(0)
    nodes, width = latent_ref.shape
    halo = halo_ref.shape[0]
    size = pre_ref.shape[0]

    @pl.when(turn == 0)
    def _():
        high, low = split(dot(halo_ref[...], wsend_ref[...]))
        table[pl.ds(0, halo), :] = high
        table[pl.ds(halo, halo), :] = low

    far = pick(block_row(send_ref, size), nodes, halo)
    pre = pre_ref[...] + dot(far, table[pl.ds(0, halo), :]) + dot(far, table[pl.ds(halo, halo), :])
    hidden, slope = swish_both(pre)
    hidden_ref[...] = hidden
    slope_ref[...] = slope
    normed, inverse = normalize(dot(hidden, w2_ref[...]))
    normed_ref[...] = normed
    inverse_ref[...] = inverse
    place = turn * size + lax.broadcasted_iota(jnp.int32, (size, 1), 0)
    message = jnp.where(place < scalar_ref[0], normed, 0.0).astype(BF)
    accumulate(gathered, dot(pick_t(block_row(recv_ref, size), 0, nodes), message))

    @pl.when(turn == pl.num_programs(0) - 1)
    def _():
        latent = latent_ref[...]
        sums = gathered[...].astype(BF)
        w_node = nw1_ref[pl.ds(0, width), :]
        w_agg = nw1_ref[pl.ds(width, width), :]
        node_hidden, node_slope = swish_both(dot(latent, w_node) + dot(sums, w_agg))
        node_normed, node_inverse = normalize(dot(node_hidden, nw2_ref[...]))
        cotan = cotan_ref[...].astype(F32)
        grad_out = norm_back(cotan, node_normed, node_inverse).astype(BF)
        grad_pre = (dot_last(grad_out, nw2_ref[...]) * node_slope).astype(BF)
        agg_ref[...] = dot_last(grad_pre, w_agg).astype(BF)
        grad_ref[...] = cotan + dot_last(grad_pre, w_node)
        acc[pl.ds(0, width), :] = dot_rows(latent, grad_pre)
        acc[pl.ds(width, width), :] = dot_rows(sums, grad_pre)
        acc[pl.ds(2 * width, width), :] = dot_rows(node_hidden, grad_out)
        stash(acc, 0, keep_ref, away_ref, scalar_ref[1])


def mixed_kernel(
    scalar_ref, recv_ref, cotan_ref, hidden_ref, normed_ref, inverse_ref, agg_ref,
    mixed_out, keep_ref, away_ref, acc,
):
    turn = pl.program_id(0)
    size = cotan_ref.shape[0]
    place = turn * size + lax.broadcasted_iota(jnp.int32, (size, 1), 0)
    grad_msg = jnp.where(
        place < scalar_ref[0],
        cotan_ref[...].astype(F32) + dot(pick(block_row(recv_ref, size), 0, agg_ref.shape[0]), agg_ref[...]),
        0.0,
    )
    grad_mixed = norm_back(grad_msg, normed_ref[...], inverse_ref[...]).astype(BF)
    mixed_out[...] = grad_mixed
    accumulate(acc, dot_rows(hidden_ref[...], grad_mixed))

    @pl.when(turn == pl.num_programs(0) - 1)
    def _():
        stash(acc, 0, keep_ref, away_ref, scalar_ref[1])


def sender_kernel(
    scalar_ref, send_ref, mixed_ref, slope_ref, w2_ref, w1_ref, grad_ref, latent_ref, halo_ref,
    pre_out, node_out, far_out, keep_ref, away_ref, sent, acc,
):
    turn = pl.program_id(0)
    nodes, width = latent_ref.shape
    halo = halo_ref.shape[0]
    grad_pre = (dot_last(mixed_ref[...], w2_ref[...]) * slope_ref[...]).astype(BF)
    pre_out[...] = grad_pre
    accumulate(sent, dot(pick_t(block_row(send_ref, mixed_ref.shape[0]), 0, nodes + halo), grad_pre))

    @pl.when(turn == pl.num_programs(0) - 1)
    def _():
        near = sent[pl.ds(0, nodes), :].astype(BF)
        far = sent[pl.ds(nodes, halo), :].astype(BF)
        far_out[...] = dot_last(far, w1_ref[...]).astype(BF)
        acc[...] = dot_rows(latent_ref[...], near) + dot_rows(halo_ref[...], far)
        stash(acc, 0, keep_ref, away_ref, scalar_ref[1])
        node_out[...] = grad_ref[...] + dot_last(near, w1_ref[...])


def receiver_kernel(
    scalar_ref, recv_ref, pre_ref, edge_ref, w1_ref, part_ref, latent_ref,
    node_out, keep_ref, away_ref, received, acc,
):
    turn = pl.program_id(0)
    nodes, width = latent_ref.shape
    grad_pre = pre_ref[...]
    accumulate(acc.at[pl.ds(width, width), :], dot_rows(edge_ref[...], grad_pre))
    accumulate(received, dot(pick_t(block_row(recv_ref, pre_ref.shape[0]), 0, nodes), grad_pre))

    @pl.when(turn == pl.num_programs(0) - 1)
    def _():
        into = received[...].astype(BF)
        acc[pl.ds(0, width), :] = dot_rows(latent_ref[...], into)
        stash(acc, 0, keep_ref, away_ref, scalar_ref[1])
        node_out[...] = part_ref[...] + dot_last(into, w1_ref[...])


def edge_kernel(cotan_ref, pre_ref, w1_ref, out_ref):
    out_ref[...] = (cotan_ref[...].astype(F32) + dot_last(pre_ref[...], w1_ref[...])).astype(BF)


def return_kernel(rows_ref, back_ref, part_ref, out_ref):
    out_ref[...] = part_ref[...] + dot(pick_t(rows_ref[...], 0, out_ref.shape[0]), back_ref[...])


def whole(shape):
    return pl.BlockSpec(shape, lambda i: (0,) * len(shape))


def by_rows(size, width):
    return pl.BlockSpec((size, width), lambda i: (i, 0))


def permute(value, pairs):
    return lax.ppermute(value, "dom", pairs).astype(F32)


def core_hop(keep, away, count):
    return keep + permute(away, [(i, i ^ 1) for i in range(count)])


def side_hop(total, count):
    groups, rows, width = total.shape
    total = total.reshape(groups // 2, 2, rows, width)
    side = (lax.axis_index("dom") // 2) % 2
    mine = lax.dynamic_index_in_dim(total, side, 1, keepdims=False)
    other = lax.dynamic_index_in_dim(total, 1 - side, 1, keepdims=False).astype(BF)
    return mine + permute(other, [(i, i ^ 2) for i in range(count)])


def group_hop(total, where, count):
    groups = count // 4
    slot = [where.index(g) if g in where else 0 for g in range(groups)]
    group = lax.axis_index("dom") // 4
    table = jnp.array(slot, jnp.int32)

    def entry(step):
        return lax.dynamic_index_in_dim(total, table[(group + step) % groups], 0, keepdims=False)

    result = entry(0)
    for step in range(1, groups):
        pairs = [(i, (i + 4 * step) % count) for i in range(count) if (i // 4 + step) % groups in where]
        result = result + permute(entry(step).astype(BF), pairs)
    return result


def local(
    count,
    node_latent,
    edge_latent,
    node_cotan,
    edge_cotan,
    edge_w1,
    edge_w2,
    node_w1,
    node_w2,
    send_rows,
    senders,
    receivers,
    edge_count,
):
    nodes, width = node_latent.shape
    edges = edge_latent.shape[0]
    peers, slots = send_rows.shape[1:]
    halo = peers * slots
    size = 512
    turns = edges // size
    place = lax.axis_index("dom")
    scalars = jnp.stack([edge_count[0], (place % 2).astype(jnp.int32)])
    flat_rows = send_rows.reshape(1, halo)
    row_spec = whole((edges,))
    smem = pl.BlockSpec(memory_space=pltpu.SMEM)
    params = pltpu.CompilerParams(vmem_limit_bytes=VMEM_BYTES)
    unit = 2 * edges * width * width

    def cost(units, bytes_accessed):
        return pl.CostEstimate(flops=int(units * unit), bytes_accessed=bytes_accessed, transcendentals=0)

    outgoing = pl.pallas_call(
        rows_kernel,
        out_shape=jax.ShapeDtypeStruct((halo, width), BF),
        compiler_params=params,
        cost_estimate=cost(0.1, 3 * halo * width * 2),
        name="halo_rows",
    )(flat_rows, node_latent)
    incoming = lax.all_to_all(
        outgoing.reshape(peers, slots, width), "dom", split_axis=0, concat_axis=0, tiled=True
    ).reshape(halo, width)

    pre = pl.pallas_call(
        early_kernel,
        grid=(turns,),
        in_specs=[row_spec, row_spec, by_rows(size, width), whole((nodes, width)), whole(edge_w1.shape)],
        out_specs=by_rows(size, width),
        out_shape=jax.ShapeDtypeStruct((edges, width), F32),
        scratch_shapes=[pltpu.VMEM((2 * nodes, width), BF)] * 2,
        compiler_params=params,
        cost_estimate=cost(5.5, edges * width * 6),
        name="edge_early",
    )(senders, receivers, edge_latent, node_latent, edge_w1)

    node_rows = 3 * width // count
    edge_rows = 4 * width // count
    hidden, slope, normed, inverse, agg_grad, grad_part, node_keep, node_away = pl.pallas_call(
        forward_kernel,
        grid=(turns,),
        in_specs=[
            smem, row_spec, row_spec, by_rows(size, width), whole((halo, width)), whole((width, width)),
            whole((width, width)), whole((nodes, width)), whole((nodes, width)),
            whole(node_w1.shape), whole(node_w2.shape),
        ],
        out_specs=[
            by_rows(size, width), by_rows(size, width), by_rows(size, width), by_rows(size, 1),
            whole((nodes, width)), whole((nodes, width)),
            whole((count // 2, node_rows, width)), whole((count // 2, node_rows, width)),
        ],
        out_shape=[
            jax.ShapeDtypeStruct((edges, width), BF),
            jax.ShapeDtypeStruct((edges, width), F32),
            jax.ShapeDtypeStruct((edges, width), F32),
            jax.ShapeDtypeStruct((edges, 1), F32),
            jax.ShapeDtypeStruct((nodes, width), BF),
            jax.ShapeDtypeStruct((nodes, width), F32),
            jax.ShapeDtypeStruct((count // 2, node_rows, width), F32),
            jax.ShapeDtypeStruct((count // 2, node_rows, width), BF),
        ],
        scratch_shapes=[
            pltpu.VMEM((2 * halo, width), BF),
            pltpu.VMEM((nodes, width), F32),
            pltpu.VMEM((3 * width, width), F32),
        ],
        compiler_params=params,
        cost_estimate=cost(6, edges * width * 20),
        name="edge_forward",
    )(
        scalars, senders, receivers, pre, incoming, edge_w1, edge_w2,
        node_latent, node_cotan, node_w1, node_w2,
    )

    half = count // 8
    kept = [jax.ShapeDtypeStruct((half, edge_rows, width), F32), jax.ShapeDtypeStruct((half, edge_rows, width), BF)]
    kept_spec = [whole((half, edge_rows, width))] * 2
    square = whole((width, width))
    per_edge = by_rows(size, width)
    node_total = core_hop(node_keep, node_away, count)

    grad_mixed, mix_keep, mix_away = pl.pallas_call(
        mixed_kernel,
        grid=(turns,),
        in_specs=[smem, row_spec, per_edge, per_edge, per_edge, by_rows(size, 1), whole((nodes, width))],
        out_specs=[per_edge] + kept_spec,
        out_shape=[jax.ShapeDtypeStruct((edges, width), BF)] + kept,
        scratch_shapes=[pltpu.VMEM((width, width), F32)],
        compiler_params=params,
        cost_estimate=cost(3, edges * width * 10),
        name="grad_mixed",
    )(scalars, receivers, edge_cotan, hidden, normed, inverse, agg_grad)

    node_total = side_hop(node_total, count)
    mix_total = core_hop(mix_keep, mix_away, count)

    grad_pre, node_part, far_grad, send_keep, send_away = pl.pallas_call(
        sender_kernel,
        grid=(turns,),
        in_specs=[
            smem, row_spec, per_edge, per_edge, square, pl.BlockSpec((width, width), lambda i: (0, 0)),
            whole((nodes, width)), whole((nodes, width)), whole((halo, width)),
        ],
        out_specs=[per_edge, whole((nodes, width)), whole((halo, width))] + kept_spec,
        out_shape=[
            jax.ShapeDtypeStruct((edges, width), BF),
            jax.ShapeDtypeStruct((nodes, width), F32),
            jax.ShapeDtypeStruct((halo, width), BF),
        ] + kept,
        scratch_shapes=[pltpu.VMEM((nodes + halo, width), F32), pltpu.VMEM((width, width), F32)],
        compiler_params=params,
        cost_estimate=cost(4, edges * width * 8),
        name="grad_pre",
    )(scalars, senders, grad_mixed, slope, edge_w2, edge_w1, grad_part, node_latent, incoming)

    returned = lax.all_to_all(
        far_grad.reshape(peers, slots, width), "dom", split_axis=0, concat_axis=0, tiled=True
    ).reshape(halo, width)
    mix_total = side_hop(mix_total, count)
    send_total = core_hop(send_keep, send_away, count)

    node_part, recv_keep, recv_away = pl.pallas_call(
        receiver_kernel,
        grid=(turns,),
        in_specs=[
            smem, row_spec, per_edge, per_edge, pl.BlockSpec((width, width), lambda i: (1, 0)),
            whole((nodes, width)), whole((nodes, width)),
        ],
        out_specs=[whole((nodes, width))] + [whole((2 * half, edge_rows, width))] * 2,
        out_shape=[
            jax.ShapeDtypeStruct((nodes, width), F32),
            jax.ShapeDtypeStruct((2 * half, edge_rows, width), F32),
            jax.ShapeDtypeStruct((2 * half, edge_rows, width), BF),
        ],
        scratch_shapes=[pltpu.VMEM((nodes, width), F32), pltpu.VMEM((2 * width, width), F32)],
        compiler_params=params,
        cost_estimate=cost(3, edges * width * 4),
        name="grad_recv",
    )(scalars, receivers, grad_pre, edge_latent, edge_w1, node_part, node_latent)

    send_total = side_hop(send_total, count)
    recv_total = core_hop(recv_keep, recv_away, count)

    grad_edge = pl.pallas_call(
        edge_kernel,
        grid=(turns,),
        in_specs=[per_edge, per_edge, pl.BlockSpec((width, width), lambda i: (2, 0))],
        out_specs=per_edge,
        out_shape=jax.ShapeDtypeStruct((edges, width), BF),
        compiler_params=params,
        cost_estimate=cost(1, edges * width * 6),
        name="grad_edge",
    )(edge_cotan, grad_pre, edge_w1)

    recv_total = side_hop(recv_total, count)
    groups = count // 4
    each = groups // 4
    inner = list(range(each, 3 * each))
    outer = list(range(each)) + list(range(3 * each, groups))
    node_share = group_hop(node_total, list(range(groups)), count)
    outer_share = group_hop(jnp.concatenate([send_total, mix_total], 0), outer, count)
    inner_share = group_hop(recv_total, inner, count)
    group = place // 4
    edge_share = jnp.where((group >= each) & (group < 3 * each), inner_share, outer_share)
    grad_node = pl.pallas_call(
        return_kernel,
        out_shape=jax.ShapeDtypeStruct((nodes, width), F32),
        compiler_params=params,
        cost_estimate=cost(0.1, nodes * width * 8),
        name="halo_return",
    )(flat_rows, returned, node_part)
    return (grad_node, grad_edge, edge_share, node_share)


def solution(mesh):
    rows = P(("member", "dom"), None)
    placed = (
        rows, rows, rows, rows, P(), P(), P(), P(), P("dom", None, None), P("dom"), P("dom"), P("dom"),
    )
    return jax.shard_map(
        functools.partial(local, mesh.shape["dom"]),
        mesh=mesh,
        in_specs=placed,
        out_specs=(rows, rows, rows, rows),
        check_vma=False,
    )
```

```python
import functools

import jax
import jax.numpy as jnp
from jax import lax
from jax.experimental import pallas as pl
from jax.experimental.pallas import tpu as pltpu
from jax.sharding import PartitionSpec as P

BF = jnp.bfloat16
F32 = jnp.float32
VMEM_BYTES = 58 * 1024 * 1024
ANY = pl.BlockSpec(memory_space=pl.ANY)
VMEM = pl.BlockSpec(memory_space=pltpu.VMEM)
SMEM = pl.BlockSpec(memory_space=pltpu.SMEM)
DMA = pltpu.SemaphoreType.DMA


def dot(left, right):
    return jnp.dot(left, right, preferred_element_type=F32)


def dot_rows(left, right):
    return lax.dot_general(left, right, (((0,), (0,)), ((), ())), preferred_element_type=F32)


def dot_last(left, right):
    return lax.dot_general(left, right, (((1,), (1,)), ((), ())), preferred_element_type=F32)


def pick(row, base, count):
    size = row.shape[1]
    column = jnp.broadcast_to(row, (128, size)).T
    wide = jnp.concatenate([column] * (count // 128), 1)
    place = lax.broadcasted_iota(jnp.int32, (size, count), 1) + base
    return jnp.where(wide == place, 1.0, 0.0).astype(BF)


def pick_t(row, base, count):
    size = row.shape[1]
    place = lax.broadcasted_iota(jnp.int32, (count, size), 0) + base
    return jnp.where(jnp.broadcast_to(row, (count, size)) == place, 1.0, 0.0).astype(BF)


def pick_slots(rows_ref, count):
    _, peers, slots = rows_ref.shape
    same = lax.broadcasted_iota(jnp.int32, (slots, slots), 0) == lax.broadcasted_iota(
        jnp.int32, (slots, slots), 1
    )
    place = lax.broadcasted_iota(jnp.int32, (slots, count), 1)
    parts = []
    for peer in range(peers):
        row = jnp.broadcast_to(rows_ref[0, peer : peer + 1, :], (slots, slots)).astype(F32)
        column = jnp.sum(jnp.where(same, row, 0.0), 1, keepdims=True).astype(jnp.int32)
        parts.append(jnp.where(column == place, 1.0, 0.0).astype(BF))
    return jnp.concatenate(parts, 0)


def normalize(mixed):
    centre = mixed - jnp.mean(mixed, -1, keepdims=True)
    inverse = lax.rsqrt(jnp.mean(centre * centre, -1, keepdims=True) + 1e-05)
    return centre * inverse, inverse


def norm_back(grad, normed, inverse):
    return inverse * (
        grad
        - jnp.mean(grad, -1, keepdims=True)
        - normed * jnp.mean(grad * normed, -1, keepdims=True)
    )


def swish_both(value):
    sig = jax.nn.sigmoid(value)
    hidden = value * sig
    return hidden.astype(BF), sig * (1.0 + value * (1.0 - sig))


def begin(source, target, sem):
    copy = pltpu.make_async_copy(source, target, sem)
    copy.start()
    return copy


class Blocks:
    def __init__(self, source, target, sems, size):
        self.source, self.target, self.sems, self.size = source, target, sems, size
        self.turns = source.shape[0] // size

    def copy(self, turn):
        rows = pl.ds(pl.multiple_of(turn * self.size, self.size), self.size)
        return pltpu.make_async_copy(self.source.at[rows, :], self.target.at[rows, :], self.sems.at[turn])

    def start(self, turn):
        self.copy(turn).start()

    def start_all(self):
        for turn in range(self.turns):
            self.start(turn)

    def wait(self, turn):
        self.copy(turn).wait()

    def wait_all(self):
        for turn in range(self.turns):
            self.wait(turn)


def to_row(column):
    return jnp.broadcast_to(column, (column.shape[0], 128)).T[0:1, :]


def to_column(row):
    return jnp.broadcast_to(row, (128, row.shape[1])).T[:, 0:1]


def block_row(ref, turn, size):
    return ref[pl.ds(pl.multiple_of(turn * size, size), size)].reshape(1, size)


def each_block(turns, body):
    def step(turn, carry):
        body(turn)
        return carry

    lax.fori_loop(0, turns, step, 0)


def rows_kernel(rows_ref, latent_ref, out_ref):
    out_ref[...] = dot(pick_slots(rows_ref, latent_ref.shape[0]), latent_ref[...]).astype(BF)


def return_kernel(rows_ref, back_ref, part_ref, out_ref):
    out_ref[...] = part_ref[...] + dot_rows(pick_slots(rows_ref, out_ref.shape[0]), back_ref[...])


def early_kernel(
    size, send_ref, recv_ref, edge_h, latent_h, w1_h, pre_h,
    edge, latent, w1, pre, table, edge_sem, out_sem, one_sem,
):
    nodes, width = latent.shape
    first = [
        begin(latent_h, latent, one_sem.at[0]),
        begin(w1_h.at[pl.ds(0, 2 * width), :], w1, one_sem.at[1]),
        begin(w1_h.at[pl.ds(2 * width, width), :], table.at[pl.ds(2 * nodes, width), :], one_sem.at[2]),
    ]
    edges = Blocks(edge_h, edge, edge_sem, size)
    outs = Blocks(pre, pre_h, out_sem, size)
    edges.start_all()
    for copy in first:
        copy.wait()
    for part in range(2):
        table[pl.ds(part * nodes, nodes), :] = dot(latent[...], w1[pl.ds(part * width, width), :]).astype(BF)

    def body(turn):
        rows = pl.ds(pl.multiple_of(turn * size, size), size)
        sender = pick(block_row(send_ref, turn, size), 0, nodes)
        receiver = pick(block_row(recv_ref, turn, size), 0, nodes)
        edges.wait(turn)
        pre[rows, :] = dot(jnp.concatenate([sender, receiver, edge[rows, :]], 1), table[...])
        outs.start(turn)

    each_block(edges.turns, body)
    outs.wait_all()


def stash(acc, keep, away, core):
    groups, rows, _ = keep.shape
    for group in range(groups):
        mine = pl.multiple_of((2 * group + core) * rows, 16)
        other = pl.multiple_of((2 * group + 1 - core) * rows, 16)
        keep[group] = acc[pl.ds(mine, rows), :]
        away[group] = acc[pl.ds(other, rows), :].astype(BF)


def forward_kernel(
    size, scalar_ref, send_ref, recv_ref, pre_h, halo_h, w1_h, w2_h, latent_h, cotan_h, nw1_h, nw2_h,
    hidden_h, slope_h, normed_h, inverse_ref, agg_h, grad_h, keep_h, away_h,
    pre, halo, wsend, w2, latent, cotan, nw1, nw2, hidden, slope, normed, agg, grad, keep, away,
    table, gathered, acc, pre_sem, out_sem, one_sem, end_sem,
):
    nodes, width = latent.shape
    far_rows = halo.shape[0]
    first = [
        begin(halo_h, halo, one_sem.at[0]),
        begin(w1_h.at[pl.ds(0, width), :], wsend, one_sem.at[1]),
    ]
    pres = Blocks(pre_h, pre, pre_sem, size)
    pres.start_all()
    second = begin(w2_h, w2, one_sem.at[2])
    later = [
        begin(source, target, one_sem.at[3 + place])
        for place, (source, target) in enumerate(
            [(latent_h, latent), (cotan_h, cotan), (nw1_h, nw1), (nw2_h, nw2)]
        )
    ]
    outs = [
        Blocks(hidden, hidden_h, out_sem.at[0], size),
        Blocks(slope, slope_h, out_sem.at[1], size),
        Blocks(normed, normed_h, out_sem.at[2], size),
    ]
    gathered[...] = jnp.zeros_like(gathered)
    for copy in first:
        copy.wait()
    table[...] = dot(halo[...], wsend[...]).astype(BF)
    second.wait()

    def body(turn):
        pres.wait(turn)
        rows = pl.ds(pl.multiple_of(turn * size, size), size)
        far = pick(block_row(send_ref, turn, size), nodes, far_rows)
        value = pre[rows, :] + dot(far, table[...])
        low_hidden, slopes = swish_both(value)
        hidden[rows, :] = low_hidden
        slope[rows, :] = slopes.astype(BF)
        unit, scale = normalize(dot(low_hidden, w2[...]))
        normed[rows, :] = unit
        inverse_ref[turn] = to_row(scale)
        for out in outs:
            out.start(turn)
        place = turn * size + lax.broadcasted_iota(jnp.int32, (size, 1), 0)
        message = jnp.where(place < scalar_ref[0], unit, 0.0).astype(BF)
        gathered[...] += dot(pick_t(block_row(recv_ref, turn, size), 0, nodes), message)

    each_block(pres.turns, body)
    for copy in later:
        copy.wait()
    sums = gathered[...].astype(BF)
    w_node = nw1[pl.ds(0, width), :]
    w_agg = nw1[pl.ds(width, width), :]
    node_hidden, node_slope = swish_both(dot(latent[...], w_node) + dot(sums, w_agg))
    node_normed, node_inverse = normalize(dot(node_hidden, nw2[...]))
    node_cotan = cotan[...].astype(F32)
    grad_out = norm_back(node_cotan, node_normed, node_inverse).astype(BF)
    acc[pl.ds(2 * width, width), :] = dot_rows(node_hidden, grad_out)
    grad_pre = (dot_last(grad_out, nw2[...]) * node_slope).astype(BF)
    agg[...] = dot_last(grad_pre, w_agg).astype(BF)
    acc[pl.ds(0, width), :] = dot_rows(latent[...], grad_pre)
    acc[pl.ds(width, width), :] = dot_rows(sums, grad_pre)
    stash(acc, keep, away, scalar_ref[1])
    grad[...] = node_cotan + dot_last(grad_pre, w_node)
    last = [
        begin(source, target, end_sem.at[place])
        for place, (source, target) in enumerate(
            [(agg, agg_h), (grad, grad_h), (keep, keep_h), (away, away_h)]
        )
    ]
    for out in outs:
        out.wait_all()
    for copy in last:
        copy.wait()


def edge_back_kernel(
    size, scalar_ref, recv_ref, inverse_ref, cotan_h, normed_h, slope_h, hidden_h, edge_h, agg_h, w2_h,
    pre_h, keep_h, away_h,
    cotan, normed, slope, hidden, edge, agg, w2, pre, keep, away,
    acc, in_sem, out_sem, one_sem, end_sem,
):
    nodes, width = agg.shape
    first = [begin(agg_h, agg, one_sem.at[0])]
    ins = [
        Blocks(source, target, in_sem.at[place], size)
        for place, (source, target) in enumerate(
            [
                (cotan_h, cotan), (normed_h, normed),
                (slope_h, slope), (hidden_h, hidden), (edge_h, edge),
            ]
        )
    ]
    turns = ins[0].turns
    for block in ins[:2]:
        block.start(0)
    first.append(begin(w2_h, w2, one_sem.at[1]))
    for block in ins[2:]:
        block.start(0)
    for turn in range(1, turns):
        for block in ins:
            block.start(turn)
    outs = Blocks(pre, pre_h, out_sem, size)
    acc[...] = jnp.zeros_like(acc)
    for copy in first:
        copy.wait()

    def body(turn):
        rows = pl.ds(pl.multiple_of(turn * size, size), size)
        place = turn * size + lax.broadcasted_iota(jnp.int32, (size, 1), 0)
        near = dot(pick(block_row(recv_ref, turn, size), 0, nodes), agg[...])
        for block in ins[:2]:
            block.wait(turn)
        grad_msg = jnp.where(place < scalar_ref[0], cotan[rows, :].astype(F32) + near, 0.0)
        grad_mixed = norm_back(grad_msg, normed[rows, :], to_column(inverse_ref[turn])).astype(BF)
        for block in ins[2:]:
            block.wait(turn)
        grad_pre = (dot_last(grad_mixed, w2[...]) * slope[rows, :].astype(F32)).astype(BF)
        pre[rows, :] = grad_pre
        outs.start(turn)
        acc[pl.ds(width, width), :] += dot_rows(hidden[rows, :], grad_mixed)
        acc[pl.ds(0, width), :] += dot_rows(edge[rows, :], grad_pre)

    each_block(turns, body)
    stash(acc, keep, away, scalar_ref[1])
    last = [begin(keep, keep_h, end_sem.at[0]), begin(away, away_h, end_sem.at[1])]
    outs.wait_all()
    for copy in last:
        copy.wait()


def scatter_kernel(
    size, scalar_ref, send_ref, recv_ref, pre_h, w1_h, part_h, latent_h, halo_h, order_h,
    node_h, far_h, keep_h, away_h,
    pre, w1, part, latent, halo, far_grad, keep, away, sent, received, acc, in_sem, one_sem, end_sem,
):
    del order_h
    nodes, width = latent.shape
    far_rows = halo.shape[0]
    ins = Blocks(pre_h, pre, in_sem, size)
    ins.start_all()
    later = [
        begin(source, target, one_sem.at[place])
        for place, (source, target) in enumerate(
            [(w1_h.at[pl.ds(0, 2 * width), :], w1), (part_h, part), (latent_h, latent), (halo_h, halo)]
        )
    ]
    sent[...] = jnp.zeros_like(sent)
    received[...] = jnp.zeros_like(received)

    def body(turn):
        ins.wait(turn)
        rows = pl.ds(pl.multiple_of(turn * size, size), size)
        sent[...] += dot(pick_t(block_row(send_ref, turn, size), 0, nodes + far_rows), pre[rows, :])
        received[...] += dot(pick_t(block_row(recv_ref, turn, size), 0, nodes), pre[rows, :])

    each_block(ins.turns, body)
    for copy in later:
        copy.wait()
    w_send = w1[pl.ds(0, width), :]
    near = sent[pl.ds(0, nodes), :].astype(BF)
    far = sent[pl.ds(nodes, far_rows), :].astype(BF)
    into = received[...].astype(BF)
    acc[pl.ds(0, width), :] = dot_rows(latent[...], near) + dot_rows(halo[...], far)
    acc[pl.ds(width, width), :] = dot_rows(latent[...], into)
    stash(acc, keep, away, scalar_ref[1])
    last = [begin(keep, keep_h, end_sem.at[0]), begin(away, away_h, end_sem.at[1])]
    far_grad[...] = dot_last(far, w_send).astype(BF)
    last.append(begin(far_grad, far_h, end_sem.at[2]))
    part[...] += dot_last(near, w_send) + dot_last(into, w1[pl.ds(width, width), :])
    last.append(begin(part, node_h, end_sem.at[3]))
    for copy in last:
        copy.wait()


def edge_kernel(size, cotan_h, pre_h, w1_h, ready0_h, ready1_h, out_h, cotan, pre, wedge, out, in_sem, out_sem, one_sem):
    del ready0_h, ready1_h
    width = wedge.shape[0]
    weight = begin(w1_h.at[pl.ds(2 * width, width), :], wedge, one_sem.at[0])
    ins = [Blocks(pre_h, pre, in_sem.at[0], size), Blocks(cotan_h, cotan, in_sem.at[1], size)]
    for turn in range(ins[0].turns):
        for block in ins:
            block.start(turn)
    outs = Blocks(out, out_h, out_sem, size)
    weight.wait()

    def body(turn):
        for block in ins:
            block.wait(turn)
        rows = pl.ds(pl.multiple_of(turn * size, size), size)
        out[rows, :] = (cotan[rows, :].astype(F32) + dot_last(pre[rows, :], wedge[...])).astype(BF)
        outs.start(turn)

    each_block(outs.turns, body)
    outs.wait_all()


def permute(value, pairs):
    return lax.ppermute(value, "dom", pairs)


class Share:
    def __init__(self, keep, away, count):
        self.count = count
        self.terms = [keep, permute(away, [(i, i ^ 1) for i in range(count)])]

    def prepare_side(self):
        side = (lax.axis_index("dom") >> 1) & 1
        paired = [t.reshape(t.shape[0] // 2, 2, *t.shape[1:]) for t in self.terms]
        mine = [lax.dynamic_index_in_dim(t, side, 1, keepdims=False) for t in paired]
        other = [lax.dynamic_index_in_dim(t, 1 - side, 1, keepdims=False) for t in paired]
        self.other = (other[0] + other[1].astype(F32)).astype(BF)
        self.terms = mine
        return self.other

    def send_side(self):
        self.terms.append(permute(self.other, [(i, i ^ 2) for i in range(self.count)]))

    def total(self):
        return sum(term.astype(F32) for term in self.terms[1:]) + self.terms[0].astype(F32)


def finish(total, count):
    groups = count // 4
    group = lax.axis_index("dom") >> 2
    result = lax.dynamic_index_in_dim(total, group, 0, keepdims=False)
    pieces = []
    for step in range(1, groups):
        piece = lax.dynamic_index_in_dim(total, (group + step) & (groups - 1), 0, keepdims=False)
        pieces.append(permute(piece.astype(BF), [(i, (i + 4 * step) % count) for i in range(count)]))
    for piece in pieces:
        result = result + piece.astype(F32)
    return result


def local(
    count,
    node_latent,
    edge_latent,
    node_cotan,
    edge_cotan,
    edge_w1,
    edge_w2,
    node_w1,
    node_w2,
    send_rows,
    senders,
    receivers,
    edge_count,
):
    nodes, width = node_latent.shape
    edges = edge_latent.shape[0]
    peers, slots = send_rows.shape[1:]
    halo = peers * slots
    size = edges // 2
    turns = edges // size
    place = lax.axis_index("dom")
    scalars = jnp.stack([edge_count[0], (place & 1).astype(jnp.int32)])
    params = pltpu.CompilerParams(vmem_limit_bytes=VMEM_BYTES)
    unit = 2 * edges * width * width

    def cost(units, bytes_accessed):
        return pl.CostEstimate(flops=int(units * unit), bytes_accessed=bytes_accessed, transcendentals=0)

    def shape(rows, dtype, columns=width):
        return jax.ShapeDtypeStruct((rows, columns), dtype)

    def stack(groups, rows, dtype):
        return jax.ShapeDtypeStruct((groups, rows, width), dtype)

    def buffer(*arrays):
        return [pltpu.VMEM(a.shape, a.dtype) for a in arrays]

    outgoing = pl.pallas_call(
        rows_kernel,
        in_specs=[VMEM, VMEM],
        out_specs=VMEM,
        out_shape=shape(halo, BF),
        compiler_params=params,
        cost_estimate=cost(0.1, 3 * halo * width * 2),
        name="halo_rows",
    )(send_rows, node_latent)
    incoming = lax.all_to_all(
        outgoing.reshape(peers, slots, width), "dom", split_axis=0, concat_axis=0, tiled=True
    ).reshape(halo, width)

    pre_shape = shape(edges, F32)
    pre = pl.pallas_call(
        functools.partial(early_kernel, size),
        in_specs=[VMEM, VMEM, ANY, ANY, ANY],
        out_specs=ANY,
        out_shape=pre_shape,
        scratch_shapes=buffer(edge_latent, node_latent, shape(2 * width, BF), pre_shape)
        + buffer(shape(2 * nodes + width, BF))
        + [DMA((turns,)), DMA((turns,)), DMA((3,))],
        compiler_params=params,
        cost_estimate=cost(3.5, edges * width * 6),
        name="edge_early",
    )(senders, receivers, edge_latent, node_latent, edge_w1)

    node_rows = 3 * width // count
    edge_rows = 4 * width // count
    half = count // 8
    square = shape(width, BF)
    state = [shape(edges, BF), shape(edges, BF), shape(edges, F32)]
    inverse_shape = jax.ShapeDtypeStruct((turns, 1, size), F32)
    ends = [
        shape(nodes, BF), shape(nodes, F32),
        stack(count // 2, node_rows, F32), stack(count // 2, node_rows, BF),
    ]
    hidden, slope, normed, inverse, agg_grad, grad_part, node_keep, node_away = pl.pallas_call(
        functools.partial(forward_kernel, size),
        in_specs=[SMEM, VMEM, VMEM] + [ANY] * 8,
        out_specs=[ANY] * 3 + [VMEM] + [ANY] * 4,
        out_shape=state + [inverse_shape] + ends,
        scratch_shapes=buffer(pre, incoming, square, edge_w2, node_latent, node_cotan, node_w1, node_w2)
        + buffer(*state, *ends)
        + buffer(shape(halo, BF), shape(nodes, F32), shape(3 * width, F32))
        + [DMA((turns,)), DMA((3, turns)), DMA((7,)), DMA((4,))],
        compiler_params=params,
        cost_estimate=cost(6, edges * width * 20),
        name="edge_forward",
    )(
        scalars, senders, receivers, pre, incoming, edge_w1, edge_w2,
        node_latent, node_cotan, node_w1, node_w2,
    )
    node_way = Share(node_keep, node_away, count)

    pre_low = shape(edges, BF)
    far_shape = shape(halo, BF)
    kept = [stack(2 * half, edge_rows, F32), stack(2 * half, edge_rows, BF)]
    two = shape(2 * width, F32)
    grad_pre, outer_keep, outer_away = pl.pallas_call(
        functools.partial(edge_back_kernel, size),
        in_specs=[SMEM, VMEM, VMEM] + [ANY] * 7,
        out_specs=[ANY] * 3,
        out_shape=[pre_low] + kept,
        scratch_shapes=buffer(
            edge_cotan, normed, slope, hidden, edge_latent, agg_grad, edge_w2, pre_low, *kept, two
        )
        + [DMA((5, turns)), DMA((turns,)), DMA((2,)), DMA((2,))],
        compiler_params=params,
        cost_estimate=cost(6, edges * width * 20),
        name="edge_backward",
    )(scalars, receivers, inverse, edge_cotan, normed, slope, hidden, edge_latent, agg_grad, edge_w2)
    order = node_way.prepare_side()
    node_way.send_side()
    outer_way = Share(outer_keep, outer_away, count)

    node_part, far_grad, inner_keep, inner_away = pl.pallas_call(
        functools.partial(scatter_kernel, size),
        in_specs=[SMEM, VMEM, VMEM] + [ANY] * 6,
        out_specs=[ANY] * 4,
        out_shape=[shape(nodes, F32), far_shape] + kept,
        scratch_shapes=buffer(pre_low, shape(2 * width, BF), grad_part, node_latent, incoming, far_shape, *kept)
        + buffer(shape(nodes + halo, F32), shape(nodes, F32), two)
        + [DMA((turns,)), DMA((4,)), DMA((4,))],
        compiler_params=params,
        cost_estimate=cost(5, edges * width * 4),
        name="edge_scatter",
    )(scalars, senders, receivers, grad_pre, edge_w1, grad_part, node_latent, incoming, order)
    inner_way = Share(inner_keep, inner_away, count)
    returned = lax.all_to_all(
        far_grad.reshape(peers, slots, width), "dom", split_axis=0, concat_axis=0, tiled=True
    ).reshape(halo, width)

    ready = [outer_way.prepare_side(), inner_way.prepare_side()]
    outer_way.send_side()
    inner_way.send_side()
    node_share = finish(node_way.total(), count)
    grad_edge = pl.pallas_call(
        functools.partial(edge_kernel, size),
        in_specs=[ANY] * 5,
        out_specs=ANY,
        out_shape=pre_low,
        scratch_shapes=buffer(edge_cotan, grad_pre, square, pre_low)
        + [DMA((2, turns)), DMA((turns,)), DMA((1,))],
        compiler_params=params,
        cost_estimate=cost(1.5, edges * width * 6),
        name="grad_edge",
    )(edge_cotan, grad_pre, edge_w1, *ready)
    edge_share = finish(jnp.concatenate([inner_way.total(), outer_way.total()], 0), count)
    grad_node = pl.pallas_call(
        return_kernel,
        in_specs=[VMEM, VMEM, VMEM],
        out_specs=VMEM,
        out_shape=shape(nodes, F32),
        compiler_params=params,
        cost_estimate=cost(0.1, nodes * width * 8),
        name="halo_return",
    )(send_rows, returned, node_part)
    return (grad_node, grad_edge, edge_share, node_share)


def solution(mesh):
    rows = P(("member", "dom"), None)
    placed = (
        rows, rows, rows, rows, P(), P(), P(), P(), P("dom", None, None), P("dom"), P("dom"), P("dom"),
    )
    return jax.shard_map(
        functools.partial(local, mesh.shape["dom"]),
        mesh=mesh,
        in_specs=placed,
        out_specs=(rows, rows, rows, rows),
        check_vma=False,
    )
```

```python
import functools

import jax
import jax.numpy as jnp
from jax import lax
from jax.experimental import pallas as pl
from jax.experimental.pallas import tpu as pltpu
from jax.sharding import PartitionSpec as P

BF = jnp.bfloat16
F32 = jnp.float32
VMEM_BYTES = 58 * 1024 * 1024
ANY = pl.BlockSpec(memory_space=pl.ANY)
VMEM = pl.BlockSpec(memory_space=pltpu.VMEM)
SMEM = pl.BlockSpec(memory_space=pltpu.SMEM)
DMA = pltpu.SemaphoreType.DMA


def dot(left, right):
    return jnp.dot(left, right, preferred_element_type=F32)


def dot_rows(left, right):
    return lax.dot_general(left, right, (((0,), (0,)), ((), ())), preferred_element_type=F32)


def dot_last(left, right):
    return lax.dot_general(left, right, (((1,), (1,)), ((), ())), preferred_element_type=F32)


def pick(row, base, count):
    size = row.shape[1]
    column = jnp.broadcast_to(row, (128, size)).T
    wide = jnp.concatenate([column] * (count // 128), 1)
    place = lax.broadcasted_iota(jnp.int32, (size, count), 1) + base
    return jnp.where(wide == place, 1.0, 0.0).astype(BF)


def pick_t(row, base, count):
    size = row.shape[1]
    place = lax.broadcasted_iota(jnp.int32, (count, size), 0) + base
    return jnp.where(jnp.broadcast_to(row, (count, size)) == place, 1.0, 0.0).astype(BF)


def pick_slots(rows_ref, count):
    _, peers, slots = rows_ref.shape
    same = lax.broadcasted_iota(jnp.int32, (slots, slots), 0) == lax.broadcasted_iota(
        jnp.int32, (slots, slots), 1
    )
    place = lax.broadcasted_iota(jnp.int32, (slots, count), 1)
    parts = []
    for peer in range(peers):
        row = jnp.broadcast_to(rows_ref[0, peer : peer + 1, :], (slots, slots)).astype(F32)
        column = jnp.sum(jnp.where(same, row, 0.0), 1, keepdims=True).astype(jnp.int32)
        parts.append(jnp.where(column == place, 1.0, 0.0).astype(BF))
    return jnp.concatenate(parts, 0)


def normalize(mixed):
    centre = mixed - jnp.mean(mixed, -1, keepdims=True)
    inverse = lax.rsqrt(jnp.mean(centre * centre, -1, keepdims=True) + 1e-05)
    return centre * inverse, inverse


def norm_back(grad, normed, inverse):
    return inverse * (
        grad
        - jnp.mean(grad, -1, keepdims=True)
        - normed * jnp.mean(grad * normed, -1, keepdims=True)
    )


def swish_both(value):
    sig = jax.nn.sigmoid(value)
    hidden = value * sig
    return hidden.astype(BF), sig * (1.0 + value * (1.0 - sig))


def begin(source, target, sem):
    copy = pltpu.make_async_copy(source, target, sem)
    copy.start()
    return copy


class Blocks:
    def __init__(self, source, target, sems, size):
        self.source, self.target, self.sems, self.size = source, target, sems, size
        self.turns = source.shape[0] // size

    def copy(self, turn):
        rows = pl.ds(pl.multiple_of(turn * self.size, self.size), self.size)
        return pltpu.make_async_copy(self.source.at[rows, :], self.target.at[rows, :], self.sems.at[turn])

    def start(self, turn):
        self.copy(turn).start()

    def start_next(self, turn):
        @pl.when(turn + 1 < self.turns)
        def _():
            self.start(turn + 1)

    def wait(self, turn):
        self.copy(turn).wait()

    def wait_all(self):
        for turn in range(self.turns):
            self.wait(turn)


def to_row(column):
    return jnp.broadcast_to(column, (column.shape[0], 128)).T[0:1, :]


def to_column(row):
    return jnp.broadcast_to(row, (128, row.shape[1])).T[:, 0:1]


def block_row(ref, turn, size):
    return ref[pl.ds(pl.multiple_of(turn * size, size), size)].reshape(1, size)


def each_block(turns, body):
    def step(turn, carry):
        body(turn)
        return carry

    lax.fori_loop(0, turns, step, 0)


def rows_kernel(rows_ref, latent_ref, out_ref):
    out_ref[...] = dot(pick_slots(rows_ref, latent_ref.shape[0]), latent_ref[...]).astype(BF)


def early_kernel(
    size, send_ref, recv_ref, edge_h, latent_h, w1_h, pre_h,
    edge, latent, w1, pre, table, edge_sem, out_sem, one_sem,
):
    nodes, width = latent.shape
    first = [
        begin(latent_h, latent, one_sem.at[0]),
        begin(w1_h.at[pl.ds(0, 2 * width), :], w1, one_sem.at[1]),
        begin(w1_h.at[pl.ds(2 * width, width), :], table.at[pl.ds(2 * nodes, width), :], one_sem.at[2]),
    ]
    edges = Blocks(edge_h, edge, edge_sem, size)
    outs = Blocks(pre, pre_h, out_sem, size)
    edges.start(0)
    for copy in first:
        copy.wait()
    for part in range(2):
        table[pl.ds(part * nodes, nodes), :] = dot(latent[...], w1[pl.ds(part * width, width), :]).astype(BF)

    def body(turn):
        rows = pl.ds(pl.multiple_of(turn * size, size), size)
        sender = pick(block_row(send_ref, turn, size), 0, nodes)
        receiver = pick(block_row(recv_ref, turn, size), 0, nodes)
        edges.wait(turn)
        edges.start_next(turn)
        pre[rows, :] = dot(jnp.concatenate([sender, receiver, edge[rows, :]], 1), table[...])
        outs.start(turn)

    each_block(edges.turns, body)
    outs.wait_all()


def stash(acc, keep, away, core):
    groups, rows, _ = keep.shape
    for group in range(groups):
        mine = pl.multiple_of((2 * group + core) * rows, 16)
        other = pl.multiple_of((2 * group + 1 - core) * rows, 16)
        keep[group] = acc[pl.ds(mine, rows), :]
        away[group] = acc[pl.ds(other, rows), :].astype(BF)


def forward_kernel(
    size, scalar_ref, send_ref, recv_ref, pre_h, halo_h, w1_h, w2_h, latent_h, cotan_h, nw1_h, nw2_h,
    hidden_h, slope_h, normed_h, inverse_ref, agg_h, grad_h, keep_h, away_h,
    pre, halo, wsend, w2, latent, cotan, nw1, nw2, hidden, slope, normed, agg, grad, keep, away,
    table, gathered, acc, pre_sem, out_sem, one_sem, end_sem,
):
    nodes, width = latent.shape
    far_rows = halo.shape[0]
    first = [
        begin(halo_h, halo, one_sem.at[0]),
        begin(w1_h.at[pl.ds(0, width), :], wsend, one_sem.at[1]),
    ]
    pres = Blocks(pre_h, pre, pre_sem, size)
    for turn in range(pres.turns):
        pres.start(turn)
    second = begin(w2_h, w2, one_sem.at[2])
    later = [
        begin(source, target, one_sem.at[3 + place])
        for place, (source, target) in enumerate(
            [(latent_h, latent), (cotan_h, cotan), (nw1_h, nw1), (nw2_h, nw2)]
        )
    ]
    outs = [
        Blocks(hidden, hidden_h, out_sem.at[0], size),
        Blocks(slope, slope_h, out_sem.at[1], size),
        Blocks(normed, normed_h, out_sem.at[2], size),
    ]
    gathered[...] = jnp.zeros_like(gathered)
    for copy in first:
        copy.wait()
    table[...] = dot(halo[...], wsend[...]).astype(BF)
    second.wait()

    def body(turn):
        pres.wait(turn)
        rows = pl.ds(pl.multiple_of(turn * size, size), size)
        far = pick(block_row(send_ref, turn, size), nodes, far_rows)
        value = pre[rows, :] + dot(far, table[...])
        low_hidden, slopes = swish_both(value)
        hidden[rows, :] = low_hidden
        slope[rows, :] = slopes.astype(BF)
        unit, scale = normalize(dot(low_hidden, w2[...]))
        normed[rows, :] = unit
        inverse_ref[turn] = to_row(scale)
        for out in outs:
            out.start(turn)
        place = turn * size + lax.broadcasted_iota(jnp.int32, (size, 1), 0)
        message = jnp.where(place < scalar_ref[0], unit, 0.0).astype(BF)
        gathered[...] += dot(pick_t(block_row(recv_ref, turn, size), 0, nodes), message)

    each_block(pres.turns, body)
    for copy in later:
        copy.wait()
    sums = gathered[...].astype(BF)
    w_node = nw1[pl.ds(0, width), :]
    w_agg = nw1[pl.ds(width, width), :]
    node_hidden, node_slope = swish_both(dot(latent[...], w_node) + dot(sums, w_agg))
    node_normed, node_inverse = normalize(dot(node_hidden, nw2[...]))
    node_cotan = cotan[...].astype(F32)
    grad_out = norm_back(node_cotan, node_normed, node_inverse).astype(BF)
    acc[pl.ds(2 * width, width), :] = dot_rows(node_hidden, grad_out)
    grad_pre = (dot_last(grad_out, nw2[...]) * node_slope).astype(BF)
    agg[...] = dot_last(grad_pre, w_agg).astype(BF)
    acc[pl.ds(0, width), :] = dot_rows(latent[...], grad_pre)
    acc[pl.ds(width, width), :] = dot_rows(sums, grad_pre)
    stash(acc, keep, away, scalar_ref[1])
    grad[...] = node_cotan + dot_last(grad_pre, w_node)
    last = [
        begin(source, target, end_sem.at[place])
        for place, (source, target) in enumerate(
            [(agg, agg_h), (grad, grad_h), (keep, keep_h), (away, away_h)]
        )
    ]
    for out in outs:
        out.wait_all()
    for copy in last:
        copy.wait()


def edge_back_kernel(
    size, scalar_ref, recv_ref, inverse_ref, cotan_h, normed_h, slope_h, hidden_h, edge_h, agg_h, w2_h,
    pre_h, keep_h, away_h,
    cotan, normed, slope, hidden, edge, agg, w2, pre, keep, away,
    acc, in_sem, out_sem, one_sem, end_sem,
):
    nodes, width = agg.shape
    first = [begin(agg_h, agg, one_sem.at[0])]
    ins = [
        Blocks(source, target, in_sem.at[place], size)
        for place, (source, target) in enumerate(
            [
                (cotan_h, cotan), (normed_h, normed),
                (slope_h, slope), (hidden_h, hidden), (edge_h, edge),
            ]
        )
    ]
    turns = ins[0].turns
    for block in ins[:2]:
        block.start(0)
    first.append(begin(w2_h, w2, one_sem.at[1]))
    outs = Blocks(pre, pre_h, out_sem, size)
    acc[...] = jnp.zeros_like(acc)
    for copy in first:
        copy.wait()

    def body(turn):
        rows = pl.ds(pl.multiple_of(turn * size, size), size)
        place = turn * size + lax.broadcasted_iota(jnp.int32, (size, 1), 0)
        near = dot(pick(block_row(recv_ref, turn, size), 0, nodes), agg[...])
        for block in ins[:2]:
            block.wait(turn)
        for block in ins[2:]:
            block.start(turn)
        grad_msg = jnp.where(place < scalar_ref[0], cotan[rows, :].astype(F32) + near, 0.0)
        grad_mixed = norm_back(grad_msg, normed[rows, :], to_column(inverse_ref[turn])).astype(BF)
        for block in ins[2:]:
            block.wait(turn)
        for block in ins[:2]:
            block.start_next(turn)
        grad_pre = (dot_last(grad_mixed, w2[...]) * slope[rows, :].astype(F32)).astype(BF)
        pre[rows, :] = grad_pre
        outs.start(turn)
        acc[pl.ds(width, width), :] += dot_rows(hidden[rows, :], grad_mixed)
        acc[pl.ds(0, width), :] += dot_rows(edge[rows, :], grad_pre)

    each_block(turns, body)
    stash(acc, keep, away, scalar_ref[1])
    last = [begin(keep, keep_h, end_sem.at[0]), begin(away, away_h, end_sem.at[1])]
    outs.wait_all()
    for copy in last:
        copy.wait()


def scatter_kernel(
    size, scalar_ref, send_ref, recv_ref, pre_h, w1_h, part_h, latent_h, halo_h, order_h,
    node_h, far_h, keep_h, away_h,
    pre, w1, part, latent, halo, far_grad, keep, away, sent, received, acc, in_sem, one_sem, end_sem,
):
    del order_h
    nodes, width = latent.shape
    far_rows = halo.shape[0]
    ins = Blocks(pre_h, pre, in_sem, size)
    ins.start(0)
    later = [
        pltpu.make_async_copy(source, target, one_sem.at[place])
        for place, (source, target) in enumerate(
            [(w1_h.at[pl.ds(0, 2 * width), :], w1), (part_h, part), (latent_h, latent), (halo_h, halo)]
        )
    ]
    sent[...] = jnp.zeros_like(sent)
    received[...] = jnp.zeros_like(received)

    def body(turn):
        ins.wait(turn)
        ins.start_next(turn)

        @pl.when(turn == ins.turns - 1)
        def _():
            for copy in later:
                copy.start()

        rows = pl.ds(pl.multiple_of(turn * size, size), size)
        sent[...] += dot(pick_t(block_row(send_ref, turn, size), 0, nodes + far_rows), pre[rows, :])
        received[...] += dot(pick_t(block_row(recv_ref, turn, size), 0, nodes), pre[rows, :])

    each_block(ins.turns, body)
    for copy in later:
        copy.wait()
    w_send = w1[pl.ds(0, width), :]
    near = sent[pl.ds(0, nodes), :].astype(BF)
    far = sent[pl.ds(nodes, far_rows), :].astype(BF)
    into = received[...].astype(BF)
    acc[pl.ds(0, width), :] = dot_rows(latent[...], near) + dot_rows(halo[...], far)
    acc[pl.ds(width, width), :] = dot_rows(latent[...], into)
    stash(acc, keep, away, scalar_ref[1])
    last = [begin(keep, keep_h, end_sem.at[0]), begin(away, away_h, end_sem.at[1])]
    far_grad[...] = dot_last(far, w_send).astype(BF)
    last.append(begin(far_grad, far_h, end_sem.at[2]))
    part[...] += dot_last(near, w_send) + dot_last(into, w1[pl.ds(width, width), :])
    last.append(begin(part, node_h, end_sem.at[3]))
    for copy in last:
        copy.wait()


def last_kernel(
    size, rows_ref, cotan_h, pre_h, w1_h, back_h, part_h, edge_h, node_h,
    cotan, pre, wedge, back, part, out, in_sem, out_sem, one_sem,
):
    width = wedge.shape[0]
    weight = begin(w1_h.at[pl.ds(2 * width, width), :], wedge, one_sem.at[0])
    ins = [Blocks(pre_h, pre, in_sem.at[0], size), Blocks(cotan_h, cotan, in_sem.at[1], size)]
    for block in ins:
        block.start(0)
    node = [begin(back_h, back, one_sem.at[1]), begin(part_h, part, one_sem.at[2])]
    outs = Blocks(out, edge_h, out_sem, size)
    slots = pick_slots(rows_ref, part.shape[0])
    weight.wait()

    def body(turn):
        for block in ins:
            block.wait(turn)
            block.start_next(turn)
        rows = pl.ds(pl.multiple_of(turn * size, size), size)
        out[rows, :] = (cotan[rows, :].astype(F32) + dot_last(pre[rows, :], wedge[...])).astype(BF)
        outs.start(turn)

    each_block(outs.turns, body)
    for copy in node:
        copy.wait()
    part[...] += dot_rows(slots, back[...])
    end = begin(part, node_h, one_sem.at[3])
    outs.wait_all()
    end.wait()


def permute(value, pairs):
    return lax.ppermute(value, "dom", pairs)


class Share:
    def __init__(self, keep, away, count):
        self.count = count
        self.terms = [keep, permute(away, [(i, i ^ 1) for i in range(count)])]

    def side_hop(self):
        side = (lax.axis_index("dom") >> 1) & 1
        paired = [t.reshape(t.shape[0] // 2, 2, *t.shape[1:]) for t in self.terms]
        mine = [lax.dynamic_index_in_dim(t, side, 1, keepdims=False) for t in paired]
        other = [lax.dynamic_index_in_dim(t, 1 - side, 1, keepdims=False) for t in paired]
        other = (other[0] + other[1].astype(F32)).astype(BF)
        self.terms = mine + [permute(other, [(i, i ^ 2) for i in range(self.count)])]
        return other

    def total(self):
        return self.terms[0] + self.terms[1].astype(F32) + self.terms[2].astype(F32)


def start_groups(total, count):
    groups = count // 4
    group = lax.axis_index("dom") >> 2
    own = lax.dynamic_index_in_dim(total, group, 0, keepdims=False)
    pieces = []
    for step in range(1, groups):
        piece = lax.dynamic_index_in_dim(total, (group + step) & (groups - 1), 0, keepdims=False)
        pieces.append(permute(piece.astype(BF), [(i, (i + 4 * step) % count) for i in range(count)]))
    return own, pieces


def end_groups(own, pieces):
    for piece in pieces:
        own = own + piece.astype(F32)
    return own


def local(
    count,
    node_latent,
    edge_latent,
    node_cotan,
    edge_cotan,
    edge_w1,
    edge_w2,
    node_w1,
    node_w2,
    send_rows,
    senders,
    receivers,
    edge_count,
):
    nodes, width = node_latent.shape
    edges = edge_latent.shape[0]
    peers, slots = send_rows.shape[1:]
    halo = peers * slots
    size = edges // 2
    turns = edges // size
    place = lax.axis_index("dom")
    scalars = jnp.stack([edge_count[0], place & 1, (place >> 1) & 1, place >> 2]).astype(jnp.int32)
    params = pltpu.CompilerParams(vmem_limit_bytes=VMEM_BYTES)
    unit = 2 * edges * width * width

    def cost(units, bytes_accessed):
        return pl.CostEstimate(flops=int(units * unit), bytes_accessed=int(bytes_accessed), transcendentals=0)

    def shape(rows, dtype, columns=width):
        return jax.ShapeDtypeStruct((rows, columns), dtype)

    def stack(groups, rows, dtype):
        return jax.ShapeDtypeStruct((groups, rows, width), dtype)

    def buffer(*arrays):
        return [pltpu.VMEM(a.shape, a.dtype) for a in arrays]

    outgoing = pl.pallas_call(
        rows_kernel,
        in_specs=[VMEM, VMEM],
        out_specs=VMEM,
        out_shape=shape(halo, BF),
        compiler_params=params,
        cost_estimate=cost(0.1, 3 * halo * width * 2),
        name="halo_rows",
    )(send_rows, node_latent)
    incoming = lax.all_to_all(
        outgoing.reshape(peers, slots, width), "dom", split_axis=0, concat_axis=0, tiled=True
    ).reshape(halo, width)

    pre_shape = shape(edges, F32)
    pre = pl.pallas_call(
        functools.partial(early_kernel, size),
        in_specs=[VMEM, VMEM, ANY, ANY, ANY],
        out_specs=ANY,
        out_shape=pre_shape,
        scratch_shapes=buffer(edge_latent, node_latent, shape(2 * width, BF), pre_shape)
        + buffer(shape(2 * nodes + width, BF))
        + [DMA((turns,)), DMA((turns,)), DMA((3,))],
        compiler_params=params,
        cost_estimate=cost(3.5, edges * width * 6),
        name="edge_early",
    )(senders, receivers, edge_latent, node_latent, edge_w1)

    node_rows = 3 * width // count
    edge_rows = 4 * width // count
    half = count // 8
    square = shape(width, BF)
    state = [shape(edges, BF), shape(edges, BF), shape(edges, F32)]
    inverse_shape = jax.ShapeDtypeStruct((turns, 1, size), F32)
    ends = [
        shape(nodes, BF), shape(nodes, F32),
        stack(count // 2, node_rows, F32), stack(count // 2, node_rows, BF),
    ]
    hidden, slope, normed, inverse, agg_grad, grad_part, node_keep, node_away = pl.pallas_call(
        functools.partial(forward_kernel, size),
        in_specs=[SMEM, VMEM, VMEM] + [ANY] * 8,
        out_specs=[ANY] * 3 + [VMEM] + [ANY] * 4,
        out_shape=state + [inverse_shape] + ends,
        scratch_shapes=buffer(pre, incoming, square, edge_w2, node_latent, node_cotan, node_w1, node_w2)
        + buffer(*state, *ends)
        + buffer(shape(halo, BF), shape(nodes, F32), shape(3 * width, F32))
        + [DMA((turns,)), DMA((3, turns)), DMA((7,)), DMA((4,))],
        compiler_params=params,
        cost_estimate=cost(6, edges * width * 20),
        name="edge_forward",
    )(
        scalars, senders, receivers, pre, incoming, edge_w1, edge_w2,
        node_latent, node_cotan, node_w1, node_w2,
    )
    node_way = Share(node_keep, node_away, count)

    pre_low = shape(edges, BF)
    far_shape = shape(halo, BF)
    kept = [stack(2 * half, edge_rows, F32), stack(2 * half, edge_rows, BF)]
    two = shape(2 * width, F32)
    grad_pre, outer_keep, outer_away = pl.pallas_call(
        functools.partial(edge_back_kernel, size),
        in_specs=[SMEM, VMEM, VMEM] + [ANY] * 7,
        out_specs=[ANY] * 3,
        out_shape=[pre_low] + kept,
        scratch_shapes=buffer(
            edge_cotan, normed, slope, hidden, edge_latent, agg_grad, edge_w2, pre_low, *kept, two
        )
        + [DMA((5, turns)), DMA((turns,)), DMA((2,)), DMA((2,))],
        compiler_params=params,
        cost_estimate=cost(6, edges * width * 20),
        name="edge_backward",
    )(scalars, receivers, inverse, edge_cotan, normed, slope, hidden, edge_latent, agg_grad, edge_w2)
    order = node_way.side_hop()
    outer_way = Share(outer_keep, outer_away, count)

    node_part, far_grad, inner_keep, inner_away = pl.pallas_call(
        functools.partial(scatter_kernel, size),
        in_specs=[SMEM, VMEM, VMEM] + [ANY] * 6,
        out_specs=[ANY] * 4,
        out_shape=[shape(nodes, F32), far_shape] + kept,
        scratch_shapes=buffer(pre_low, shape(2 * width, BF), grad_part, node_latent, incoming, far_shape, *kept)
        + buffer(shape(nodes + halo, F32), shape(nodes, F32), two)
        + [DMA((turns,)), DMA((4,)), DMA((4,))],
        compiler_params=params,
        cost_estimate=cost(5, edges * width * 4),
        name="edge_scatter",
    )(scalars, senders, receivers, grad_pre, edge_w1, grad_part, node_latent, incoming, order)
    inner_way = Share(inner_keep, inner_away, count)
    outer_way.side_hop()
    ready = inner_way.side_hop()
    far_grad, _ = lax.optimization_barrier((far_grad, ready))
    node_own, node_pieces = start_groups(node_way.total(), count)
    returned = lax.all_to_all(
        far_grad.reshape(peers, slots, width), "dom", split_axis=0, concat_axis=0, tiled=True
    ).reshape(halo, width)
    edge_own, edge_pieces = start_groups(jnp.concatenate([inner_way.total(), outer_way.total()], 0), count)

    grad_edge, grad_node = pl.pallas_call(
        functools.partial(last_kernel, size),
        in_specs=[VMEM] + [ANY] * 5,
        out_specs=[ANY] * 2,
        out_shape=[pre_low, shape(nodes, F32)],
        scratch_shapes=buffer(edge_cotan, grad_pre, square, far_shape, shape(nodes, F32), pre_low)
        + [DMA((2, turns)), DMA((turns,)), DMA((4,))],
        compiler_params=params,
        cost_estimate=cost(1.5, edges * width * 6),
        name="last_grads",
    )(send_rows, edge_cotan, grad_pre, edge_w1, returned, node_part)
    node_share = end_groups(node_own, node_pieces)
    edge_own, grad_node = lax.optimization_barrier((edge_own, grad_node))
    edge_share = end_groups(edge_own, edge_pieces)
    return (grad_node, grad_edge, edge_share, node_share)


def solution(mesh):
    rows = P(("member", "dom"), None)
    placed = (
        rows, rows, rows, rows, P(), P(), P(), P(), P("dom", None, None), P("dom"), P("dom"), P("dom"),
    )
    return jax.shard_map(
        functools.partial(local, mesh.shape["dom"]),
        mesh=mesh,
        in_specs=placed,
        out_specs=(rows, rows, rows, rows),
        check_vma=False,
    )
```

```python
import functools

import jax
import jax.numpy as jnp
from jax import lax
from jax.experimental import pallas as pl
from jax.experimental.pallas import tpu as pltpu
from jax.sharding import PartitionSpec as P

BF = jnp.bfloat16
F32 = jnp.float32
VMEM_BYTES = 58 * 1024 * 1024
SMALL_BYTES = 52 * 1024 * 1024
ANY = pl.BlockSpec(memory_space=pl.ANY)
VMEM = pl.BlockSpec(memory_space=pltpu.VMEM)
SMEM = pl.BlockSpec(memory_space=pltpu.SMEM)
DMA = pltpu.SemaphoreType.DMA


def dot(left, right):
    return jnp.dot(left, right, preferred_element_type=F32)


def dot_rows(left, right):
    return lax.dot_general(left, right, (((0,), (0,)), ((), ())), preferred_element_type=F32)


def dot_last(left, right):
    return lax.dot_general(left, right, (((1,), (1,)), ((), ())), preferred_element_type=F32)


def pick(row, base, count):
    size = row.shape[1]
    column = jnp.broadcast_to(row, (128, size)).T
    wide = jnp.concatenate([column] * (count // 128), 1)
    place = lax.broadcasted_iota(jnp.int32, (size, count), 1) + base
    return jnp.where(wide == place, 1.0, 0.0).astype(BF)


def pick_t(row, base, count):
    size = row.shape[1]
    place = lax.broadcasted_iota(jnp.int32, (count, size), 0) + base
    return jnp.where(jnp.broadcast_to(row, (count, size)) == place, 1.0, 0.0).astype(BF)


def pick_slots(rows_ref, count):
    _, peers, slots = rows_ref.shape
    same = lax.broadcasted_iota(jnp.int32, (slots, slots), 0) == lax.broadcasted_iota(
        jnp.int32, (slots, slots), 1
    )
    place = lax.broadcasted_iota(jnp.int32, (slots, count), 1)
    parts = []
    for peer in range(peers):
        row = jnp.broadcast_to(rows_ref[0, peer : peer + 1, :], (slots, slots)).astype(F32)
        column = jnp.sum(jnp.where(same, row, 0.0), 1, keepdims=True).astype(jnp.int32)
        parts.append(jnp.where(column == place, 1.0, 0.0).astype(BF))
    return jnp.concatenate(parts, 0)


def normalize(mixed):
    centre = mixed - jnp.mean(mixed, -1, keepdims=True)
    inverse = lax.rsqrt(jnp.mean(centre * centre, -1, keepdims=True) + 1e-05)
    return centre * inverse, inverse


def norm_back(grad, normed, inverse):
    return inverse * (
        grad
        - jnp.mean(grad, -1, keepdims=True)
        - normed * jnp.mean(grad * normed, -1, keepdims=True)
    )


def swish_both(value):
    sig = jax.nn.sigmoid(value)
    hidden = value * sig
    return hidden.astype(BF), sig * (1.0 + value * (1.0 - sig))


def begin(source, target, sem):
    copy = pltpu.make_async_copy(source, target, sem)
    copy.start()
    return copy


class Blocks:
    def __init__(self, source, target, sems, size):
        self.source, self.target, self.sems, self.size = source, target, sems, size
        self.turns = source.shape[0] // size

    def copy(self, turn):
        rows = pl.ds(pl.multiple_of(turn * self.size, self.size), self.size)
        return pltpu.make_async_copy(self.source.at[rows, :], self.target.at[rows, :], self.sems.at[turn])

    def start(self, turn):
        self.copy(turn).start()

    def start_next(self, turn):
        @pl.when(turn + 1 < self.turns)
        def _():
            self.start(turn + 1)

    def wait(self, turn):
        self.copy(turn).wait()

    def wait_all(self):
        for turn in range(self.turns):
            self.wait(turn)


def to_row(column):
    return jnp.broadcast_to(column, (column.shape[0], 128)).T[0:1, :]


def to_column(row):
    return jnp.broadcast_to(row, (128, row.shape[1])).T[:, 0:1]


def block_row(ref, turn, size):
    return ref[pl.ds(pl.multiple_of(turn * size, size), size)].reshape(1, size)


def each_block(turns, body):
    for turn in range(turns):
        body(turn)


def rows_kernel(rows_ref, latent_ref, out_ref):
    out_ref[...] = dot(pick_slots(rows_ref, latent_ref.shape[0]), latent_ref[...]).astype(BF)


def early_kernel(
    size, send_ref, recv_ref, edge_h, latent_h, w1_h, pre_h,
    edge, latent, w1, pre, table, edge_sem, out_sem, one_sem,
):
    nodes, width = latent.shape
    first = [
        begin(latent_h, latent, one_sem.at[0]),
        begin(w1_h.at[pl.ds(0, 2 * width), :], w1, one_sem.at[1]),
        begin(w1_h.at[pl.ds(2 * width, width), :], table.at[pl.ds(2 * nodes, width), :], one_sem.at[2]),
    ]
    edges = Blocks(edge_h, edge, edge_sem, size)
    outs = Blocks(pre, pre_h, out_sem, size)
    edges.start(0)
    for copy in first:
        copy.wait()
    for part in range(2):
        table[pl.ds(part * nodes, nodes), :] = dot(latent[...], w1[pl.ds(part * width, width), :]).astype(BF)

    def body(turn):
        rows = pl.ds(pl.multiple_of(turn * size, size), size)
        sender = pick(block_row(send_ref, turn, size), 0, nodes)
        receiver = pick(block_row(recv_ref, turn, size), 0, nodes)
        edges.wait(turn)
        edges.start_next(turn)
        pre[rows, :] = dot(jnp.concatenate([sender, receiver, edge[rows, :]], 1), table[...])
        outs.start(turn)

    each_block(edges.turns, body)
    outs.wait_all()


def stash(acc, keep, away, core):
    groups, rows, _ = keep.shape
    for group in range(groups):
        mine = pl.multiple_of((2 * group + core) * rows, 16)
        other = pl.multiple_of((2 * group + 1 - core) * rows, 16)
        keep[group] = acc[pl.ds(mine, rows), :]
        away[group] = acc[pl.ds(other, rows), :].astype(BF)


def forward_kernel(
    size, scalar_ref, send_ref, recv_ref, pre_h, halo_h, w1_h, w2_h, latent_h, cotan_h, nw1_h, nw2_h,
    hidden_h, slope_h, normed_h, inverse_ref, agg_h, grad_h, keep_h, away_h,
    pre, halo, wsend, w2, latent, cotan, nw1, nw2, hidden, slope, normed, agg, grad, keep, away,
    table, gathered, acc, pre_sem, out_sem, one_sem, end_sem,
):
    nodes, width = latent.shape
    far_rows = halo.shape[0]
    first = [
        begin(halo_h, halo, one_sem.at[0]),
        begin(w1_h.at[pl.ds(0, width), :], wsend, one_sem.at[1]),
    ]
    pres = Blocks(pre_h, pre, pre_sem, size)
    for turn in range(pres.turns):
        pres.start(turn)
    second = begin(w2_h, w2, one_sem.at[2])
    later = [
        begin(source, target, one_sem.at[3 + place])
        for place, (source, target) in enumerate(
            [(latent_h, latent), (cotan_h, cotan), (nw1_h, nw1), (nw2_h, nw2)]
        )
    ]
    outs = [
        Blocks(hidden, hidden_h, out_sem.at[0], size),
        Blocks(slope, slope_h, out_sem.at[1], size),
        Blocks(normed, normed_h, out_sem.at[2], size),
    ]
    gathered[...] = jnp.zeros_like(gathered)
    for copy in first:
        copy.wait()
    table[...] = dot(halo[...], wsend[...]).astype(BF)
    second.wait()

    def body(turn):
        pres.wait(turn)
        rows = pl.ds(pl.multiple_of(turn * size, size), size)
        far = pick(block_row(send_ref, turn, size), nodes, far_rows)
        value = pre[rows, :] + dot(far, table[...])
        low_hidden, slopes = swish_both(value)
        hidden[rows, :] = low_hidden
        slope[rows, :] = slopes.astype(BF)
        unit, scale = normalize(dot(low_hidden, w2[...]))
        normed[rows, :] = unit
        inverse_ref[turn] = to_row(scale)
        for out in outs:
            out.start(turn)
        place = turn * size + lax.broadcasted_iota(jnp.int32, (size, 1), 0)
        message = jnp.where(place < scalar_ref[0], unit, 0.0).astype(BF)
        gathered[...] += dot(pick_t(block_row(recv_ref, turn, size), 0, nodes), message)

    each_block(pres.turns, body)
    for copy in later:
        copy.wait()
    sums = gathered[...].astype(BF)
    w_node = nw1[pl.ds(0, width), :]
    w_agg = nw1[pl.ds(width, width), :]
    node_hidden, node_slope = swish_both(dot(latent[...], w_node) + dot(sums, w_agg))
    node_normed, node_inverse = normalize(dot(node_hidden, nw2[...]))
    node_cotan = cotan[...].astype(F32)
    grad_out = norm_back(node_cotan, node_normed, node_inverse).astype(BF)
    acc[pl.ds(2 * width, width), :] = dot_rows(node_hidden, grad_out)
    grad_pre = (dot_last(grad_out, nw2[...]) * node_slope).astype(BF)
    agg[...] = dot_last(grad_pre, w_agg).astype(BF)
    acc[pl.ds(0, width), :] = dot_rows(latent[...], grad_pre)
    acc[pl.ds(width, width), :] = dot_rows(sums, grad_pre)
    stash(acc, keep, away, scalar_ref[1])
    grad[...] = node_cotan + dot_last(grad_pre, w_node)
    last = [
        begin(source, target, end_sem.at[place])
        for place, (source, target) in enumerate(
            [(agg, agg_h), (grad, grad_h), (keep, keep_h), (away, away_h)]
        )
    ]
    for out in outs:
        out.wait_all()
    for copy in last:
        copy.wait()


def edge_back_kernel(
    size, scalar_ref, recv_ref, inverse_ref, cotan_h, normed_h, slope_h, hidden_h, edge_h, agg_h, w2_h,
    pre_h, keep_h, away_h,
    cotan, normed, slope, hidden, edge, agg, w2, pre, keep, away,
    acc, in_sem, out_sem, one_sem, end_sem,
):
    nodes, width = agg.shape
    first = [begin(agg_h, agg, one_sem.at[0])]
    ins = [
        Blocks(source, target, in_sem.at[place], size)
        for place, (source, target) in enumerate(
            [
                (cotan_h, cotan), (normed_h, normed),
                (slope_h, slope), (hidden_h, hidden), (edge_h, edge),
            ]
        )
    ]
    turns = ins[0].turns
    for block in ins[:2]:
        block.start(0)
    first.append(begin(w2_h, w2, one_sem.at[1]))
    outs = Blocks(pre, pre_h, out_sem, size)
    acc[...] = jnp.zeros_like(acc)
    for copy in first:
        copy.wait()

    def body(turn):
        rows = pl.ds(pl.multiple_of(turn * size, size), size)
        place = turn * size + lax.broadcasted_iota(jnp.int32, (size, 1), 0)
        near = dot(pick(block_row(recv_ref, turn, size), 0, nodes), agg[...])
        for block in ins[:2]:
            block.wait(turn)
        for block in ins[2:]:
            block.start(turn)
        grad_msg = jnp.where(place < scalar_ref[0], cotan[rows, :].astype(F32) + near, 0.0)
        grad_mixed = norm_back(grad_msg, normed[rows, :], to_column(inverse_ref[turn])).astype(BF)
        for block in ins[2:]:
            block.wait(turn)
        for block in ins[:2]:
            block.start_next(turn)
        grad_pre = (dot_last(grad_mixed, w2[...]) * slope[rows, :].astype(F32)).astype(BF)
        pre[rows, :] = grad_pre
        outs.start(turn)
        acc[pl.ds(width, width), :] += dot_rows(hidden[rows, :], grad_mixed)
        acc[pl.ds(0, width), :] += dot_rows(edge[rows, :], grad_pre)

    each_block(turns, body)
    stash(acc, keep, away, scalar_ref[1])
    last = [begin(keep, keep_h, end_sem.at[0]), begin(away, away_h, end_sem.at[1])]
    outs.wait_all()
    for copy in last:
        copy.wait()


def scatter_kernel(
    size, scalar_ref, send_ref, recv_ref, pre_h, w1_h, part_h, latent_h, halo_h, order_h,
    node_h, far_h, keep_h, away_h,
    pre, w1, part, latent, halo, far_grad, keep, away, sent, received, acc, in_sem, one_sem, end_sem,
):
    del order_h
    nodes, width = latent.shape
    far_rows = halo.shape[0]
    ins = Blocks(pre_h, pre, in_sem, size)
    ins.start(0)
    later = [
        pltpu.make_async_copy(source, target, one_sem.at[place])
        for place, (source, target) in enumerate(
            [(w1_h.at[pl.ds(0, 2 * width), :], w1), (part_h, part), (latent_h, latent), (halo_h, halo)]
        )
    ]
    sent[...] = jnp.zeros_like(sent)
    received[...] = jnp.zeros_like(received)

    def body(turn):
        ins.wait(turn)
        ins.start_next(turn)

        @pl.when(turn == ins.turns - 1)
        def _():
            for copy in later:
                copy.start()

        rows = pl.ds(pl.multiple_of(turn * size, size), size)
        sent[...] += dot(pick_t(block_row(send_ref, turn, size), 0, nodes + far_rows), pre[rows, :])
        received[...] += dot(pick_t(block_row(recv_ref, turn, size), 0, nodes), pre[rows, :])

    each_block(ins.turns, body)
    for copy in later:
        copy.wait()
    w_send = w1[pl.ds(0, width), :]
    near = sent[pl.ds(0, nodes), :].astype(BF)
    far = sent[pl.ds(nodes, far_rows), :].astype(BF)
    into = received[...].astype(BF)
    acc[pl.ds(0, width), :] = dot_rows(latent[...], near) + dot_rows(halo[...], far)
    acc[pl.ds(width, width), :] = dot_rows(latent[...], into)
    stash(acc, keep, away, scalar_ref[1])
    last = [begin(keep, keep_h, end_sem.at[0]), begin(away, away_h, end_sem.at[1])]
    far_grad[...] = dot_last(far, w_send).astype(BF)
    last.append(begin(far_grad, far_h, end_sem.at[2]))
    part[...] += dot_last(near, w_send) + dot_last(into, w1[pl.ds(width, width), :])
    last.append(begin(part, node_h, end_sem.at[3]))
    for copy in last:
        copy.wait()


def last_kernel(
    size, rows_ref, cotan_h, pre_h, w1_h, back_h, part_h, edge_h, node_h,
    cotan, pre, wedge, back, part, out, in_sem, out_sem, one_sem,
):
    width = wedge.shape[0]
    weight = begin(w1_h.at[pl.ds(2 * width, width), :], wedge, one_sem.at[0])
    ins = [Blocks(pre_h, pre, in_sem.at[0], size), Blocks(cotan_h, cotan, in_sem.at[1], size)]
    for block in ins:
        block.start(0)
    node = [begin(back_h, back, one_sem.at[1]), begin(part_h, part, one_sem.at[2])]
    outs = Blocks(out, edge_h, out_sem, size)
    slots = pick_slots(rows_ref, part.shape[0])
    weight.wait()

    def body(turn):
        for block in ins:
            block.wait(turn)
            block.start_next(turn)
        rows = pl.ds(pl.multiple_of(turn * size, size), size)
        out[rows, :] = (cotan[rows, :].astype(F32) + dot_last(pre[rows, :], wedge[...])).astype(BF)
        outs.start(turn)

    each_block(outs.turns, body)
    for copy in node:
        copy.wait()
    part[...] += dot_rows(slots, back[...])
    end = begin(part, node_h, one_sem.at[3])
    outs.wait_all()
    end.wait()


def permute(value, pairs):
    return lax.ppermute(value, "dom", pairs)


class Share:
    def __init__(self, keep, away, count):
        self.count = count
        self.terms = [keep, permute(away, [(i, i ^ 1) for i in range(count)])]

    def side_hop(self):
        side = (lax.axis_index("dom") >> 1) & 1
        paired = [t.reshape(t.shape[0] // 2, 2, *t.shape[1:]) for t in self.terms]
        mine = [lax.dynamic_index_in_dim(t, side, 1, keepdims=False) for t in paired]
        other = [lax.dynamic_index_in_dim(t, 1 - side, 1, keepdims=False) for t in paired]
        other = (other[0] + other[1].astype(F32)).astype(BF)
        self.terms = mine + [permute(other, [(i, i ^ 2) for i in range(self.count)])]
        return other

    def total(self):
        return self.terms[0] + self.terms[1].astype(F32) + self.terms[2].astype(F32)


def start_groups(total, count):
    groups = count // 4
    group = lax.axis_index("dom") >> 2
    own = lax.dynamic_index_in_dim(total, group, 0, keepdims=False)
    pieces = []
    for step in range(1, groups):
        piece = lax.dynamic_index_in_dim(total, (group + step) & (groups - 1), 0, keepdims=False)
        pieces.append(permute(piece.astype(BF), [(i, (i + 4 * step) % count) for i in range(count)]))
    return own, pieces


def end_groups(own, pieces):
    for piece in pieces:
        own = own + piece.astype(F32)
    return own


def local(
    count,
    node_latent,
    edge_latent,
    node_cotan,
    edge_cotan,
    edge_w1,
    edge_w2,
    node_w1,
    node_w2,
    send_rows,
    senders,
    receivers,
    edge_count,
):
    nodes, width = node_latent.shape
    edges = edge_latent.shape[0]
    peers, slots = send_rows.shape[1:]
    halo = peers * slots
    size = edges // 2
    turns = edges // size
    place = lax.axis_index("dom")
    scalars = jnp.stack([edge_count[0], place & 1, (place >> 1) & 1, place >> 2]).astype(jnp.int32)
    params = pltpu.CompilerParams(vmem_limit_bytes=VMEM_BYTES)
    small = pltpu.CompilerParams(vmem_limit_bytes=SMALL_BYTES)
    unit = 2 * edges * width * width

    def cost(units, bytes_accessed):
        return pl.CostEstimate(flops=int(units * unit), bytes_accessed=int(bytes_accessed), transcendentals=0)

    def shape(rows, dtype, columns=width):
        return jax.ShapeDtypeStruct((rows, columns), dtype)

    def stack(groups, rows, dtype):
        return jax.ShapeDtypeStruct((groups, rows, width), dtype)

    def buffer(*arrays):
        return [pltpu.VMEM(a.shape, a.dtype) for a in arrays]

    outgoing = pl.pallas_call(
        rows_kernel,
        in_specs=[VMEM, VMEM],
        out_specs=VMEM,
        out_shape=shape(halo, BF),
        compiler_params=params,
        cost_estimate=cost(0.1, 3 * halo * width * 2),
        name="halo_rows",
    )(send_rows, node_latent)
    incoming = lax.all_to_all(
        outgoing.reshape(peers, slots, width), "dom", split_axis=0, concat_axis=0, tiled=True
    ).reshape(halo, width)

    pre_shape = shape(edges, F32)
    pre = pl.pallas_call(
        functools.partial(early_kernel, size),
        in_specs=[VMEM, VMEM, ANY, ANY, ANY],
        out_specs=ANY,
        out_shape=pre_shape,
        scratch_shapes=buffer(edge_latent, node_latent, shape(2 * width, BF), pre_shape)
        + buffer(shape(2 * nodes + width, BF))
        + [DMA((turns,)), DMA((turns,)), DMA((3,))],
        compiler_params=params,
        cost_estimate=cost(3.5, edges * width * 6),
        name="edge_early",
    )(senders, receivers, edge_latent, node_latent, edge_w1)

    node_rows = 3 * width // count
    edge_rows = 4 * width // count
    half = count // 8
    square = shape(width, BF)
    state = [shape(edges, BF), shape(edges, BF), shape(edges, F32)]
    inverse_shape = jax.ShapeDtypeStruct((turns, 1, size), F32)
    ends = [
        shape(nodes, BF), shape(nodes, F32),
        stack(count // 2, node_rows, F32), stack(count // 2, node_rows, BF),
    ]
    hidden, slope, normed, inverse, agg_grad, grad_part, node_keep, node_away = pl.pallas_call(
        functools.partial(forward_kernel, size),
        in_specs=[SMEM, VMEM, VMEM] + [ANY] * 8,
        out_specs=[ANY] * 3 + [VMEM] + [ANY] * 4,
        out_shape=state + [inverse_shape] + ends,
        scratch_shapes=buffer(pre, incoming, square, edge_w2, node_latent, node_cotan, node_w1, node_w2)
        + buffer(*state, *ends)
        + buffer(shape(halo, BF), shape(nodes, F32), shape(3 * width, F32))
        + [DMA((turns,)), DMA((3, turns)), DMA((7,)), DMA((4,))],
        compiler_params=small,
        cost_estimate=cost(6, edges * width * 20),
        name="edge_forward",
    )(
        scalars, senders, receivers, pre, incoming, edge_w1, edge_w2,
        node_latent, node_cotan, node_w1, node_w2,
    )
    node_way = Share(node_keep, node_away, count)

    pre_low = shape(edges, BF)
    far_shape = shape(halo, BF)
    kept = [stack(2 * half, edge_rows, F32), stack(2 * half, edge_rows, BF)]
    two = shape(2 * width, F32)
    grad_pre, outer_keep, outer_away = pl.pallas_call(
        functools.partial(edge_back_kernel, size),
        in_specs=[SMEM, VMEM, VMEM] + [ANY] * 7,
        out_specs=[ANY] * 3,
        out_shape=[pre_low] + kept,
        scratch_shapes=buffer(
            edge_cotan, normed, slope, hidden, edge_latent, agg_grad, edge_w2, pre_low, *kept, two
        )
        + [DMA((5, turns)), DMA((turns,)), DMA((2,)), DMA((2,))],
        compiler_params=small,
        cost_estimate=cost(6, edges * width * 20),
        name="edge_backward",
    )(scalars, receivers, inverse, edge_cotan, normed, slope, hidden, edge_latent, agg_grad, edge_w2)
    order = node_way.side_hop()
    outer_way = Share(outer_keep, outer_away, count)

    node_part, far_grad, inner_keep, inner_away = pl.pallas_call(
        functools.partial(scatter_kernel, size),
        in_specs=[SMEM, VMEM, VMEM] + [ANY] * 6,
        out_specs=[ANY] * 4,
        out_shape=[shape(nodes, F32), far_shape] + kept,
        scratch_shapes=buffer(pre_low, shape(2 * width, BF), grad_part, node_latent, incoming, far_shape, *kept)
        + buffer(shape(nodes + halo, F32), shape(nodes, F32), two)
        + [DMA((turns,)), DMA((4,)), DMA((4,))],
        compiler_params=small,
        cost_estimate=cost(5, edges * width * 4),
        name="edge_scatter",
    )(scalars, senders, receivers, grad_pre, edge_w1, grad_part, node_latent, incoming, order)
    inner_way = Share(inner_keep, inner_away, count)
    outer_way.side_hop()
    ready = inner_way.side_hop()
    far_grad, _ = lax.optimization_barrier((far_grad, ready))
    node_own, node_pieces = start_groups(node_way.total(), count)
    returned = lax.all_to_all(
        far_grad.reshape(peers, slots, width), "dom", split_axis=0, concat_axis=0, tiled=True
    ).reshape(halo, width)
    edge_own, edge_pieces = start_groups(jnp.concatenate([inner_way.total(), outer_way.total()], 0), count)

    grad_edge, grad_node = pl.pallas_call(
        functools.partial(last_kernel, size),
        in_specs=[VMEM] + [ANY] * 5,
        out_specs=[ANY] * 2,
        out_shape=[pre_low, shape(nodes, F32)],
        scratch_shapes=buffer(edge_cotan, grad_pre, square, far_shape, shape(nodes, F32), pre_low)
        + [DMA((2, turns)), DMA((turns,)), DMA((4,))],
        compiler_params=small,
        cost_estimate=cost(1.5, edges * width * 6),
        name="last_grads",
    )(send_rows, edge_cotan, grad_pre, edge_w1, returned, node_part)
    node_share = end_groups(node_own, node_pieces)
    edge_own, grad_node = lax.optimization_barrier((edge_own, grad_node))
    edge_share = end_groups(edge_own, edge_pieces)
    return (grad_node, grad_edge, edge_share, node_share)


def solution(mesh):
    rows = P(("member", "dom"), None)
    placed = (
        rows, rows, rows, rows, P(), P(), P(), P(), P("dom", None, None), P("dom"), P("dom"), P("dom"),
    )
    return jax.shard_map(
        functools.partial(local, mesh.shape["dom"]),
        mesh=mesh,
        in_specs=placed,
        out_specs=(rows, rows, rows, rows),
        check_vma=False,
    )
```

```python
import functools

import jax
import jax.numpy as jnp
from jax import lax
from jax.experimental import pallas as pl
from jax.experimental.pallas import tpu as pltpu
from jax.sharding import PartitionSpec as P

BF = jnp.bfloat16
F32 = jnp.float32
VMEM_BYTES = 58 * 1024 * 1024
SMALL_BYTES = 52 * 1024 * 1024
ANY = pl.BlockSpec(memory_space=pl.ANY)
VMEM = pl.BlockSpec(memory_space=pltpu.VMEM)
SMEM = pl.BlockSpec(memory_space=pltpu.SMEM)
DMA = pltpu.SemaphoreType.DMA


def dot(left, right):
    return jnp.dot(left, right, preferred_element_type=F32)


def dot_rows(left, right):
    return lax.dot_general(left, right, (((0,), (0,)), ((), ())), preferred_element_type=F32)


def dot_last(left, right):
    return lax.dot_general(left, right, (((1,), (1,)), ((), ())), preferred_element_type=F32)


def pick(row, base, count):
    size = row.shape[1]
    column = jnp.broadcast_to(row, (128, size)).T
    wide = jnp.concatenate([column] * (count // 128), 1)
    place = lax.broadcasted_iota(jnp.int32, (size, count), 1) + base
    return jnp.where(wide == place, 1.0, 0.0).astype(BF)


def pick_t(row, base, count):
    size = row.shape[1]
    place = lax.broadcasted_iota(jnp.int32, (count, size), 0) + base
    return jnp.where(jnp.broadcast_to(row, (count, size)) == place, 1.0, 0.0).astype(BF)


def pick_slots(rows_ref, count):
    _, peers, slots = rows_ref.shape
    same = lax.broadcasted_iota(jnp.int32, (slots, slots), 0) == lax.broadcasted_iota(
        jnp.int32, (slots, slots), 1
    )
    place = lax.broadcasted_iota(jnp.int32, (slots, count), 1)
    parts = []
    for peer in range(peers):
        row = jnp.broadcast_to(rows_ref[0, peer : peer + 1, :], (slots, slots)).astype(F32)
        column = jnp.sum(jnp.where(same, row, 0.0), 1, keepdims=True).astype(jnp.int32)
        parts.append(jnp.where(column == place, 1.0, 0.0).astype(BF))
    return jnp.concatenate(parts, 0)


def normalize(mixed):
    centre = mixed - jnp.mean(mixed, -1, keepdims=True)
    inverse = lax.rsqrt(jnp.mean(centre * centre, -1, keepdims=True) + 1e-05)
    return centre * inverse, inverse


def norm_back(grad, normed, inverse):
    return inverse * (
        grad
        - jnp.mean(grad, -1, keepdims=True)
        - normed * jnp.mean(grad * normed, -1, keepdims=True)
    )


def swish_both(value):
    sig = jax.nn.sigmoid(value)
    hidden = value * sig
    return hidden.astype(BF), sig * (1.0 + value * (1.0 - sig))


def begin(source, target, sem):
    copy = pltpu.make_async_copy(source, target, sem)
    copy.start()
    return copy


class Blocks:
    def __init__(self, source, target, sems, size):
        self.source, self.target, self.sems, self.size = source, target, sems, size
        self.turns = source.shape[0] // size

    def copy(self, turn):
        rows = pl.ds(pl.multiple_of(turn * self.size, self.size), self.size)
        return pltpu.make_async_copy(self.source.at[rows, :], self.target.at[rows, :], self.sems.at[turn])

    def start(self, turn):
        self.copy(turn).start()

    def start_next(self, turn):
        @pl.when(turn + 1 < self.turns)
        def _():
            self.start(turn + 1)

    def wait(self, turn):
        self.copy(turn).wait()

    def wait_all(self):
        for turn in range(self.turns):
            self.wait(turn)


def to_row(column):
    return jnp.broadcast_to(column, (column.shape[0], 128)).T[0:1, :]


def to_column(row):
    return jnp.broadcast_to(row, (128, row.shape[1])).T[:, 0:1]


def block_row(ref, turn, size):
    return ref[pl.ds(pl.multiple_of(turn * size, size), size)].reshape(1, size)


def add_block(ref, value, turn):
    ref[...] = value if turn == 0 else ref[...] + value


def each_block(turns, body):
    for turn in range(turns):
        body(turn)


def rows_kernel(rows_ref, latent_ref, out_ref):
    out_ref[...] = dot(pick_slots(rows_ref, latent_ref.shape[0]), latent_ref[...]).astype(BF)


def early_kernel(
    size, send_ref, recv_ref, edge_h, latent_h, w1_h, pre_h,
    edge, latent, w1, pre, table, edge_sem, out_sem, one_sem,
):
    nodes, width = latent.shape
    first = [
        begin(latent_h, latent, one_sem.at[0]),
        begin(w1_h.at[pl.ds(0, 2 * width), :], w1, one_sem.at[1]),
        begin(w1_h.at[pl.ds(2 * width, width), :], table.at[pl.ds(2 * nodes, width), :], one_sem.at[2]),
    ]
    edges = Blocks(edge_h, edge, edge_sem, size)
    outs = Blocks(pre, pre_h, out_sem, size)
    edges.start(0)
    for copy in first:
        copy.wait()
    for part in range(2):
        table[pl.ds(part * nodes, nodes), :] = dot(latent[...], w1[pl.ds(part * width, width), :]).astype(BF)

    def body(turn):
        rows = pl.ds(pl.multiple_of(turn * size, size), size)
        sender = pick(block_row(send_ref, turn, size), 0, nodes)
        receiver = pick(block_row(recv_ref, turn, size), 0, nodes)
        edges.wait(turn)
        edges.start_next(turn)
        pre[rows, :] = dot(jnp.concatenate([sender, receiver, edge[rows, :]], 1), table[...])
        outs.start(turn)

    each_block(edges.turns, body)
    outs.wait_all()


def stash(acc, keep, away, core):
    groups, rows, _ = keep.shape
    for group in range(groups):
        mine = pl.multiple_of((2 * group + core) * rows, 16)
        other = pl.multiple_of((2 * group + 1 - core) * rows, 16)
        keep[group] = acc[pl.ds(mine, rows), :]
        away[group] = acc[pl.ds(other, rows), :].astype(BF)


def forward_kernel(
    size, scalar_ref, send_ref, recv_ref, pre_h, halo_h, w1_h, w2_h, latent_h, cotan_h, nw1_h, nw2_h,
    hidden_h, slope_h, normed_h, inverse_ref, agg_h, grad_h, keep_h, away_h,
    pre, halo, wsend, w2, latent, cotan, nw1, nw2, hidden, slope, normed, agg, grad, keep, away,
    table, gathered, acc, pre_sem, out_sem, one_sem, end_sem,
):
    nodes, width = latent.shape
    far_rows = halo.shape[0]
    first = [
        begin(halo_h, halo, one_sem.at[0]),
        begin(w1_h.at[pl.ds(0, width), :], wsend, one_sem.at[1]),
    ]
    pres = Blocks(pre_h, pre, pre_sem, size)
    for turn in range(pres.turns):
        pres.start(turn)
    second = begin(w2_h, w2, one_sem.at[2])
    later = [
        begin(source, target, one_sem.at[3 + place])
        for place, (source, target) in enumerate(
            [(latent_h, latent), (cotan_h, cotan), (nw1_h, nw1), (nw2_h, nw2)]
        )
    ]
    outs = [
        Blocks(hidden, hidden_h, out_sem.at[0], size),
        Blocks(slope, slope_h, out_sem.at[1], size),
        Blocks(normed, normed_h, out_sem.at[2], size),
    ]
    for copy in first:
        copy.wait()
    table[...] = dot(halo[...], wsend[...]).astype(BF)
    second.wait()

    def body(turn):
        pres.wait(turn)
        rows = pl.ds(pl.multiple_of(turn * size, size), size)
        far = pick(block_row(send_ref, turn, size), nodes, far_rows)
        value = pre[rows, :] + dot(far, table[...])
        low_hidden, slopes = swish_both(value)
        hidden[rows, :] = low_hidden
        slope[rows, :] = slopes.astype(BF)
        unit, scale = normalize(dot(low_hidden, w2[...]))
        normed[rows, :] = unit
        inverse_ref[turn] = to_row(scale)
        for out in outs:
            out.start(turn)
        place = turn * size + lax.broadcasted_iota(jnp.int32, (size, 1), 0)
        message = jnp.where(place < scalar_ref[0], unit, 0.0).astype(BF)
        add_block(gathered, dot(pick_t(block_row(recv_ref, turn, size), 0, nodes), message), turn)

    each_block(pres.turns, body)
    for copy in later:
        copy.wait()
    sums = gathered[...].astype(BF)
    w_node = nw1[pl.ds(0, width), :]
    w_agg = nw1[pl.ds(width, width), :]
    node_hidden, node_slope = swish_both(dot(latent[...], w_node) + dot(sums, w_agg))
    node_normed, node_inverse = normalize(dot(node_hidden, nw2[...]))
    node_cotan = cotan[...].astype(F32)
    grad_out = norm_back(node_cotan, node_normed, node_inverse).astype(BF)
    acc[pl.ds(2 * width, width), :] = dot_rows(node_hidden, grad_out)
    grad_pre = (dot_last(grad_out, nw2[...]) * node_slope).astype(BF)
    agg[...] = dot_last(grad_pre, w_agg).astype(BF)
    acc[pl.ds(0, width), :] = dot_rows(latent[...], grad_pre)
    acc[pl.ds(width, width), :] = dot_rows(sums, grad_pre)
    stash(acc, keep, away, scalar_ref[1])
    grad[...] = node_cotan + dot_last(grad_pre, w_node)
    last = [
        begin(source, target, end_sem.at[place])
        for place, (source, target) in enumerate(
            [(agg, agg_h), (grad, grad_h), (keep, keep_h), (away, away_h)]
        )
    ]
    for out in outs:
        out.wait_all()
    for copy in last:
        copy.wait()


def edge_back_kernel(
    size, scalar_ref, recv_ref, inverse_ref, cotan_h, normed_h, slope_h, hidden_h, edge_h, agg_h, w2_h,
    pre_h, keep_h, away_h,
    cotan, normed, slope, hidden, edge, agg, w2, pre, keep, away,
    acc, in_sem, out_sem, one_sem, end_sem,
):
    nodes, width = agg.shape
    first = [begin(agg_h, agg, one_sem.at[0])]
    ins = [
        Blocks(source, target, in_sem.at[place], size)
        for place, (source, target) in enumerate(
            [
                (cotan_h, cotan), (normed_h, normed),
                (slope_h, slope), (hidden_h, hidden), (edge_h, edge),
            ]
        )
    ]
    turns = ins[0].turns
    for block in ins[:2]:
        block.start(0)
    first.append(begin(w2_h, w2, one_sem.at[1]))
    outs = Blocks(pre, pre_h, out_sem, size)
    for copy in first:
        copy.wait()

    def body(turn):
        rows = pl.ds(pl.multiple_of(turn * size, size), size)
        place = turn * size + lax.broadcasted_iota(jnp.int32, (size, 1), 0)
        near = dot(pick(block_row(recv_ref, turn, size), 0, nodes), agg[...])
        for block in ins[:2]:
            block.wait(turn)
        for block in ins[2:]:
            block.start(turn)
        grad_msg = jnp.where(place < scalar_ref[0], cotan[rows, :].astype(F32) + near, 0.0)
        grad_mixed = norm_back(grad_msg, normed[rows, :], to_column(inverse_ref[turn])).astype(BF)
        for block in ins[2:]:
            block.wait(turn)
        for block in ins[:2]:
            block.start_next(turn)
        grad_pre = (dot_last(grad_mixed, w2[...]) * slope[rows, :].astype(F32)).astype(BF)
        pre[rows, :] = grad_pre
        outs.start(turn)
        add_block(acc.at[pl.ds(width, width), :], dot_rows(hidden[rows, :], grad_mixed), turn)
        add_block(acc.at[pl.ds(0, width), :], dot_rows(edge[rows, :], grad_pre), turn)

    each_block(turns, body)
    stash(acc, keep, away, scalar_ref[1])
    last = [begin(keep, keep_h, end_sem.at[0]), begin(away, away_h, end_sem.at[1])]
    outs.wait_all()
    for copy in last:
        copy.wait()


def scatter_kernel(
    size, scalar_ref, send_ref, recv_ref, pre_h, w1_h, part_h, latent_h, halo_h, order_h,
    node_h, far_h, keep_h, away_h,
    pre, w1, part, latent, halo, far_grad, keep, away, sums, acc, in_sem, one_sem, end_sem,
):
    del order_h
    nodes, width = latent.shape
    far_rows = halo.shape[0]
    ins = Blocks(pre_h, pre, in_sem, size)
    ins.start(0)
    later = [
        pltpu.make_async_copy(source, target, one_sem.at[place])
        for place, (source, target) in enumerate(
            [(w1_h.at[pl.ds(0, 2 * width), :], w1), (part_h, part), (latent_h, latent), (halo_h, halo)]
        )
    ]

    def body(turn):
        ins.wait(turn)
        ins.start_next(turn)

        @pl.when(turn == ins.turns - 1)
        def _():
            for copy in later:
                copy.start()

        rows = pl.ds(pl.multiple_of(turn * size, size), size)
        both = jnp.concatenate(
            [
                pick_t(block_row(send_ref, turn, size), 0, nodes + far_rows),
                pick_t(block_row(recv_ref, turn, size), 0, nodes),
            ],
            0,
        )
        add_block(sums, dot(both, pre[rows, :]), turn)

    each_block(ins.turns, body)
    for copy in later:
        copy.wait()
    w_send = w1[pl.ds(0, width), :]
    near = sums[pl.ds(0, nodes), :].astype(BF)
    far = sums[pl.ds(nodes, far_rows), :].astype(BF)
    into = sums[pl.ds(nodes + far_rows, nodes), :].astype(BF)
    acc[pl.ds(0, width), :] = dot_rows(latent[...], near) + dot_rows(halo[...], far)
    acc[pl.ds(width, width), :] = dot_rows(latent[...], into)
    stash(acc, keep, away, scalar_ref[1])
    last = [begin(keep, keep_h, end_sem.at[0]), begin(away, away_h, end_sem.at[1])]
    far_grad[...] = dot_last(far, w_send).astype(BF)
    last.append(begin(far_grad, far_h, end_sem.at[2]))
    part[...] += dot_last(near, w_send) + dot_last(into, w1[pl.ds(width, width), :])
    last.append(begin(part, node_h, end_sem.at[3]))
    for copy in last:
        copy.wait()


def last_kernel(
    size, rows_ref, cotan_h, pre_h, w1_h, back_h, part_h, edge_h, node_h,
    cotan, pre, wedge, back, part, out, in_sem, out_sem, one_sem,
):
    width = wedge.shape[0]
    weight = begin(w1_h.at[pl.ds(2 * width, width), :], wedge, one_sem.at[0])
    ins = [Blocks(pre_h, pre, in_sem.at[0], size), Blocks(cotan_h, cotan, in_sem.at[1], size)]
    for block in ins:
        block.start(0)
    node = [begin(back_h, back, one_sem.at[1]), begin(part_h, part, one_sem.at[2])]
    outs = Blocks(out, edge_h, out_sem, size)
    slots = pick_slots(rows_ref, part.shape[0])
    weight.wait()

    def body(turn):
        for block in ins:
            block.wait(turn)
            block.start_next(turn)
        rows = pl.ds(pl.multiple_of(turn * size, size), size)
        out[rows, :] = (cotan[rows, :].astype(F32) + dot_last(pre[rows, :], wedge[...])).astype(BF)
        outs.start(turn)

    each_block(outs.turns, body)
    for copy in node:
        copy.wait()
    part[...] += dot_rows(slots, back[...])
    end = begin(part, node_h, one_sem.at[3])
    outs.wait_all()
    end.wait()


def permute(value, pairs):
    return lax.ppermute(value, "dom", pairs)


class Share:
    def __init__(self, keep, away, count):
        self.count = count
        self.terms = [keep, permute(away, [(i, i ^ 1) for i in range(count)])]

    def side_hop(self):
        side = (lax.axis_index("dom") >> 1) & 1
        paired = [t.reshape(t.shape[0] // 2, 2, *t.shape[1:]) for t in self.terms]
        mine = [lax.dynamic_index_in_dim(t, side, 1, keepdims=False) for t in paired]
        other = [lax.dynamic_index_in_dim(t, 1 - side, 1, keepdims=False) for t in paired]
        other = (other[0] + other[1].astype(F32)).astype(BF)
        self.terms = mine + [permute(other, [(i, i ^ 2) for i in range(self.count)])]
        return other

    def total(self):
        return self.terms[0] + self.terms[1].astype(F32) + self.terms[2].astype(F32)


def start_groups(total, count):
    groups = count // 4
    group = lax.axis_index("dom") >> 2
    own = lax.dynamic_index_in_dim(total, group, 0, keepdims=False)
    pieces = []
    for step in range(1, groups):
        piece = lax.dynamic_index_in_dim(total, (group + step) & (groups - 1), 0, keepdims=False)
        pieces.append(permute(piece.astype(BF), [(i, (i + 4 * step) % count) for i in range(count)]))
    return own, pieces


def end_groups(own, pieces):
    for piece in pieces:
        own = own + piece.astype(F32)
    return own


def local(
    count,
    node_latent,
    edge_latent,
    node_cotan,
    edge_cotan,
    edge_w1,
    edge_w2,
    node_w1,
    node_w2,
    send_rows,
    senders,
    receivers,
    edge_count,
):
    nodes, width = node_latent.shape
    edges = edge_latent.shape[0]
    peers, slots = send_rows.shape[1:]
    halo = peers * slots
    size = edges // 2
    turns = edges // size
    place = lax.axis_index("dom")
    scalars = jnp.stack([edge_count[0], place & 1, (place >> 1) & 1, place >> 2]).astype(jnp.int32)
    params = pltpu.CompilerParams(vmem_limit_bytes=VMEM_BYTES)
    small = pltpu.CompilerParams(vmem_limit_bytes=SMALL_BYTES)
    unit = 2 * edges * width * width

    def cost(units, bytes_accessed):
        return pl.CostEstimate(flops=int(units * unit), bytes_accessed=int(bytes_accessed), transcendentals=0)

    def shape(rows, dtype, columns=width):
        return jax.ShapeDtypeStruct((rows, columns), dtype)

    def stack(groups, rows, dtype):
        return jax.ShapeDtypeStruct((groups, rows, width), dtype)

    def buffer(*arrays):
        return [pltpu.VMEM(a.shape, a.dtype) for a in arrays]

    outgoing = pl.pallas_call(
        rows_kernel,
        in_specs=[VMEM, VMEM],
        out_specs=VMEM,
        out_shape=shape(halo, BF),
        compiler_params=params,
        cost_estimate=cost(0.1, 3 * halo * width * 2),
        name="halo_rows",
    )(send_rows, node_latent)
    incoming = lax.all_to_all(
        outgoing.reshape(peers, slots, width), "dom", split_axis=0, concat_axis=0, tiled=True
    ).reshape(halo, width)

    pre_shape = shape(edges, F32)
    pre = pl.pallas_call(
        functools.partial(early_kernel, size),
        in_specs=[VMEM, VMEM, ANY, ANY, ANY],
        out_specs=ANY,
        out_shape=pre_shape,
        scratch_shapes=buffer(edge_latent, node_latent, shape(2 * width, BF), pre_shape)
        + buffer(shape(2 * nodes + width, BF))
        + [DMA((turns,)), DMA((turns,)), DMA((3,))],
        compiler_params=params,
        cost_estimate=cost(3.5, edges * width * 6),
        name="edge_early",
    )(senders, receivers, edge_latent, node_latent, edge_w1)

    node_rows = 3 * width // count
    edge_rows = 4 * width // count
    half = count // 8
    square = shape(width, BF)
    state = [shape(edges, BF), shape(edges, BF), shape(edges, F32)]
    inverse_shape = jax.ShapeDtypeStruct((turns, 1, size), F32)
    ends = [
        shape(nodes, BF), shape(nodes, F32),
        stack(count // 2, node_rows, F32), stack(count // 2, node_rows, BF),
    ]
    hidden, slope, normed, inverse, agg_grad, grad_part, node_keep, node_away = pl.pallas_call(
        functools.partial(forward_kernel, size),
        in_specs=[SMEM, VMEM, VMEM] + [ANY] * 8,
        out_specs=[ANY] * 3 + [VMEM] + [ANY] * 4,
        out_shape=state + [inverse_shape] + ends,
        scratch_shapes=buffer(pre, incoming, square, edge_w2, node_latent, node_cotan, node_w1, node_w2)
        + buffer(*state, *ends)
        + buffer(shape(halo, BF), shape(nodes, F32), shape(3 * width, F32))
        + [DMA((turns,)), DMA((3, turns)), DMA((7,)), DMA((4,))],
        compiler_params=small,
        cost_estimate=cost(6, edges * width * 20),
        name="edge_forward",
    )(
        scalars, senders, receivers, pre, incoming, edge_w1, edge_w2,
        node_latent, node_cotan, node_w1, node_w2,
    )
    node_way = Share(node_keep, node_away, count)

    pre_low = shape(edges, BF)
    far_shape = shape(halo, BF)
    kept = [stack(2 * half, edge_rows, F32), stack(2 * half, edge_rows, BF)]
    two = shape(2 * width, F32)
    grad_pre, outer_keep, outer_away = pl.pallas_call(
        functools.partial(edge_back_kernel, size),
        in_specs=[SMEM, VMEM, VMEM] + [ANY] * 7,
        out_specs=[ANY] * 3,
        out_shape=[pre_low] + kept,
        scratch_shapes=buffer(
            edge_cotan, normed, slope, hidden, edge_latent, agg_grad, edge_w2, pre_low, *kept, two
        )
        + [DMA((5, turns)), DMA((turns,)), DMA((2,)), DMA((2,))],
        compiler_params=small,
        cost_estimate=cost(6, edges * width * 20),
        name="edge_backward",
    )(scalars, receivers, inverse, edge_cotan, normed, slope, hidden, edge_latent, agg_grad, edge_w2)
    order = node_way.side_hop()
    outer_way = Share(outer_keep, outer_away, count)

    node_part, far_grad, inner_keep, inner_away = pl.pallas_call(
        functools.partial(scatter_kernel, size),
        in_specs=[SMEM, VMEM, VMEM] + [ANY] * 6,
        out_specs=[ANY] * 4,
        out_shape=[shape(nodes, F32), far_shape] + kept,
        scratch_shapes=buffer(pre_low, shape(2 * width, BF), grad_part, node_latent, incoming, far_shape, *kept)
        + buffer(shape(2 * nodes + halo, F32), two)
        + [DMA((turns,)), DMA((4,)), DMA((4,))],
        compiler_params=pltpu.CompilerParams(vmem_limit_bytes=50 * 1024 * 1024),
        cost_estimate=cost(5, edges * width * 4),
        name="edge_scatter",
    )(scalars, senders, receivers, grad_pre, edge_w1, grad_part, node_latent, incoming, order)
    inner_way = Share(inner_keep, inner_away, count)
    outer_way.side_hop()
    ready = inner_way.side_hop()
    far_grad, _ = lax.optimization_barrier((far_grad, ready))
    node_own, node_pieces = start_groups(node_way.total(), count)
    returned = lax.all_to_all(
        far_grad.reshape(peers, slots, width), "dom", split_axis=0, concat_axis=0, tiled=True
    ).reshape(halo, width)
    edge_own, edge_pieces = start_groups(jnp.concatenate([inner_way.total(), outer_way.total()], 0), count)

    grad_edge, grad_node = pl.pallas_call(
        functools.partial(last_kernel, size),
        in_specs=[VMEM] + [ANY] * 5,
        out_specs=[ANY] * 2,
        out_shape=[pre_low, shape(nodes, F32)],
        scratch_shapes=buffer(edge_cotan, grad_pre, square, far_shape, shape(nodes, F32), pre_low)
        + [DMA((2, turns)), DMA((turns,)), DMA((4,))],
        compiler_params=small,
        cost_estimate=cost(1.5, edges * width * 6),
        name="last_grads",
    )(send_rows, edge_cotan, grad_pre, edge_w1, returned, node_part)
    node_share = end_groups(node_own, node_pieces)
    edge_own, grad_node = lax.optimization_barrier((edge_own, grad_node))
    edge_share = end_groups(edge_own, edge_pieces)
    return (grad_node, grad_edge, edge_share, node_share)


def solution(mesh):
    rows = P(("member", "dom"), None)
    placed = (
        rows, rows, rows, rows, P(), P(), P(), P(), P("dom", None, None), P("dom"), P("dom"), P("dom"),
    )
    return jax.shard_map(
        functools.partial(local, mesh.shape["dom"]),
        mesh=mesh,
        in_specs=placed,
        out_specs=(rows, rows, rows, rows),
        check_vma=False,
    )
```
